128 devices in a mesh: seq: 8 (over z, core), enc: 4 (over x), dp: 4 (over y).
Axes of the slice: x: 4, y: 4, z: 4, core: 2. Of those that a mesh axis runs over, the one named last changes fastest.
Arguments:
- tokens: bfloat16 [2048, 4096], P(('seq', 'enc', 'dp')), may hold values from -6 to 6
- cotangent: bfloat16 [2048, 4096], P(('seq', 'enc', 'dp')), may hold values from -6 to 6
- encoded: bfloat16 [128, 128, 4096], P('seq'), may hold values from -6 to 6
- w_query: bfloat16 [4096, 2048], P(None, ('enc', 'dp')), may hold values from -0.09375 to 0.09375
- w_key: bfloat16 [4096, 2048], P(None, ('enc', 'dp')), may hold values from -0.09375 to 0.09375
- w_value: bfloat16 [4096, 2048], P(None, ('enc', 'dp')), may hold values from -0.09375 to 0.09375
- w_out: bfloat16 [2048, 4096], P(('enc', 'dp')), may hold values from -0.5 to 0.5
- neigh_owner: int32 [32, 2], replicated, may hold values from 0 to 7, all different within a row; in each aligned block of 4 rows (0 to 3, 4 to 7, ...) at most 2 rows name the same one
- neigh_row: int32 [32, 2], replicated, may hold values from 0 to 15
Outputs:
- block_out: bfloat16 [2048, 4096], P(('seq', 'enc', 'dp'))
- grad_tokens: bfloat16 [2048, 4096], P(('seq', 'enc', 'dp'))
- grad_query: bfloat16 [4096, 2048], P('seq', ('enc', 'dp'))
- grad_key: bfloat16 [4096, 2048], P('seq', ('enc', 'dp'))
- grad_value: bfloat16 [4096, 2048], P('seq', ('enc', 'dp'))
- grad_out: bfloat16 [2048, 4096], P(('enc', 'dp'), 'seq')
The draws below stay inside these ranges and needn't reach their ends.
Inputs may be any that keep to these rules, and one draw needn't show every extreme that they name: `neigh_owner`: the 2 owners of a group differ. Among the groups of one index of seq (aligned blocks of 4 rows) no owner is named more than 2 times, a bound that some block reaches.
All inputs are finite; a program needn't handle non-finite values.
Results may differ from the reference program's by a relative error of at most 0.02.
Values may be sent and summed in bfloat16 or wider, within the bound.
A program may use at most 128 MiB of HBM per device.

```python
import math
import jax
import jax.numpy as jnp
import numpy as np
from jax import lax

D = 4096
HEAD_DIM = 128
GROUP = 64
NLEN = 128
NEIGH = 2
SEQ_LEN = 2048
CH_DEV = 4
NB_OWN = 16
HEADS = 16
HD = 2048
GROUPS = 32
TOKENS = 2048
NBLK = 128
CAP = 2
N_SEQ = 8


def plant(drawn, rng, low, top_value):
    place = [jax.random.randint(jax.random.fold_in(rng, axis), (), 0, length) for axis, length in enumerate(drawn.shape)]
    longest = drawn.shape.index(max(drawn.shape))
    next_to = place[:longest] + [(place[longest] + 1) % drawn.shape[longest]] + place[longest + 1:]
    return drawn.at[tuple(place)].set(low).at[tuple(next_to)].set(top_value)


def level_of(key, extent, split, low, top_value):
    def one(position, parts):
        draws = jax.random.uniform(jax.random.fold_in(jax.random.fold_in(key, 6), position), (parts,), jnp.float32, low / len(split), top_value / len(split))
        return jnp.repeat(jnp.exp(draws), extent[position] // parts).reshape((-1,) + (1,) * (len(extent) - position - 1))

    loudness = one(*split[0])
    for cut in split[1:]:
        loudness = loudness * one(*cut)
    return loudness


def assign_block(key, own, number, rows, number_of, top, reach, skew):
    order = jax.random.permutation(key, number_of)
    packed, common = load_shares(number_of, rows * top, reach, skew, True), load_shares(number_of, rows * top, reach, skew, False)
    places = jnp.arange(number_of)

    def named(sizes, rotation):
        used = int((sizes > 0).sum())
        fixed = max(1, used // 4)
        moved = fixed + (places - fixed + rotation * (used - fixed)) % max(1, number_of - fixed)
        return jnp.zeros((number_of,), jnp.int32).at[order[jnp.where(places < fixed, places, moved)]].set(jnp.asarray(sizes, jnp.int32))

    sizes = jnp.where(number % 4 == 0, named(packed, number // 4), named(common, number - number // 4 - 1))
    mixed = jax.random.permutation(jax.random.fold_in(own, 3), number_of)
    donor, receiver = mixed[0:number_of // 2 * 2:2], mixed[1:number_of // 2 * 2:2]
    room = jnp.minimum(sizes[donor] - 1, reach - sizes[receiver]) // 2
    room = jnp.where((donor == order[0]) | (receiver == order[0]) | (sizes[receiver] == 0), 0, jnp.maximum(room, 0))
    moved = jax.random.randint(jax.random.fold_in(own, 4), (number_of // 2,), 0, 1 << 20) % (room + 1)
    sizes = sizes.at[donor].add(-moved).at[receiver].add(moved)
    labels = jnp.searchsorted(jnp.cumsum(sizes), jnp.arange(rows * top), side="right").astype(jnp.int32)
    grid = labels.reshape(top, rows).T
    grid = grid[jax.random.permutation(jax.random.fold_in(own, 1), rows)]
    rotation = jax.random.randint(jax.random.fold_in(own, 2), (rows, 1), 0, top)
    return jnp.take_along_axis(grid, (jnp.arange(top)[None, :] + rotation) % top, axis=1)


def load_shares(number_of, total, most, slope, full):
    weights = [(1 << 20) // math.isqrt(grade ** slope) + 1 for grade in range(1, number_of + 1)]
    largest = most if full else min(most, max(-(-total // number_of), total * weights[0] // sum(weights)))
    least = 1 if total - largest >= number_of - 1 else 0
    given, rest = [largest] + [least] * (number_of - 1), total - largest - least * (number_of - 1)
    while rest > 0:
        movable = [i for i in range(1, number_of) if given[i] < largest] or [i for i in range(1, number_of) if given[i] < most]
        mass, left = sum([weights[i] for i in movable]), rest
        for i in movable:
            extra = min(most - given[i], max(1, left * weights[i] // mass), rest)
            given[i] = given[i] + extra
            rest = rest - extra
    return np.array(given)


def bell_draw(rng, dims, deviation, limit, shards=(), kind=jnp.bfloat16):
    loudness = level_of(rng, dims, shards, -0.22, 0.18) if shards else 1.0
    drawn = jax.random.normal(rng, dims, jnp.float32) * deviation * loudness
    return jnp.minimum(jnp.maximum(drawn, -limit), limit).astype(kind)


def setup_inputs(seed: int = 0) -> dict:
    key_of = jax.random.split(jax.random.key(seed), 10)
    tokens = bell_draw(key_of[0], (TOKENS, D), 1.0, 6.0, ((0, 128),))
    cotangent = bell_draw(key_of[1], (TOKENS, D), 1.0, 6.0, ((0, 128),))
    encoded = bell_draw(key_of[2], (NBLK, NLEN, D), 1.0, 6.0, ((0, 8),))
    w_query = bell_draw(key_of[3], (D, HD), D ** -0.5, 0.09375, ((1, 16),))
    w_key = bell_draw(key_of[4], (D, HD), D ** -0.5, 0.09375, ((1, 16),))
    w_value = bell_draw(key_of[5], (D, HD), D ** -0.5, 0.09375, ((1, 16),))
    w_out = bell_draw(key_of[6], (HD, D), (HD // 16) ** -0.5, 0.5, ((0, 16),))
    neigh_owner_keys = jax.random.split(jax.random.fold_in(key_of[7], 1), GROUPS // CH_DEV)
    neigh_owner_turns = jax.random.permutation(jax.random.fold_in(key_of[7], 3), GROUPS // CH_DEV)
    neigh_owner = jax.vmap(lambda own, number: assign_block(jax.random.fold_in(key_of[7], 2), own, number, CH_DEV, N_SEQ, NEIGH, CAP, 2))(neigh_owner_keys, neigh_owner_turns).reshape((GROUPS, NEIGH))
    neigh_row = plant(jax.random.randint(key_of[8], (GROUPS, NEIGH), 0, NB_OWN), jax.random.fold_in(key_of[8], 1), 0, NB_OWN - 1).astype(jnp.int32)
    return {"tokens": tokens, "cotangent": cotangent, "encoded": encoded, "w_query": w_query, "w_key": w_key, "w_value": w_value, "w_out": w_out, "neigh_owner": neigh_owner, "neigh_row": neigh_row}


def attend(queries, kv_prev, kv_cur, last_row, live_mask):
    head_dim = queries.shape[-1]
    score_scale = 1.0 / math.sqrt(head_dim)
    query_full = queries.astype(jnp.float32)
    keys_prev = kv_prev[..., :head_dim].astype(jnp.float32)
    vals_prev = kv_prev[..., head_dim:].astype(jnp.float32)
    keys_cur = kv_cur[..., :head_dim].astype(jnp.float32)
    vals_cur = kv_cur[..., head_dim:].astype(jnp.float32)
    pick = last_row[None, :, None]
    scores = jnp.where(pick, jnp.einsum('cqd,ckd->cqk', query_full, keys_cur), jnp.einsum('cqd,ckd->cqk', query_full, keys_prev)) * score_scale
    row_peak = lax.optimization_barrier(jnp.max(scores, axis=-1, keepdims=True))
    expos = jnp.exp(scores - row_peak)
    attn_probs = expos / lax.optimization_barrier(jnp.sum(expos, axis=-1, keepdims=True))
    probs_half = attn_probs.astype(jnp.bfloat16)
    probs_full = probs_half.astype(jnp.float32)
    mixed_vals = jnp.where(pick, jnp.einsum('cqk,ckd->cqd', probs_full, vals_cur), jnp.einsum('cqk,ckd->cqd', probs_full, vals_prev))
    attn = (mixed_vals * live_mask[..., None]).astype(jnp.bfloat16)
    return (attn, attn_probs, probs_half)

def attend_back(queries, kv_prev, kv_cur, last_row, attn_probs, probs_half, d_attn):
    head_dim = queries.shape[-1]
    score_scale = 1.0 / math.sqrt(head_dim)
    query_full = queries.astype(jnp.float32)
    keys_prev = kv_prev[..., :head_dim].astype(jnp.float32)
    vals_prev = kv_prev[..., head_dim:].astype(jnp.float32)
    keys_cur = kv_cur[..., :head_dim].astype(jnp.float32)
    vals_cur = kv_cur[..., head_dim:].astype(jnp.float32)
    pick = last_row[None, :, None]
    grad_full = d_attn.astype(jnp.float32)
    grad_probs = jnp.where(pick, jnp.einsum('cqd,ckd->cqk', grad_full, vals_cur), jnp.einsum('cqd,ckd->cqk', grad_full, vals_prev))
    row_delta = lax.optimization_barrier(jnp.sum(attn_probs * grad_probs, axis=-1, keepdims=True))
    d_scores = (attn_probs * (grad_probs - row_delta) * score_scale).astype(jnp.bfloat16)
    score_full = d_scores.astype(jnp.float32)
    d_queries = jnp.where(pick, jnp.einsum('cqk,ckd->cqd', score_full, keys_cur), jnp.einsum('cqk,ckd->cqd', score_full, keys_prev)).astype(jnp.bfloat16)
    last_full = last_row.astype(jnp.float32)[None, :, None]
    other_full = 1.0 - last_full
    probs_full = probs_half.astype(jnp.float32)
    grad_prev = jnp.concatenate([jnp.einsum('cqk,cqd->ckd', score_full * other_full, query_full), jnp.einsum('cqk,cqd->ckd', probs_full * other_full, grad_full)], axis=-1)
    grad_cur = jnp.concatenate([jnp.einsum('cqk,cqd->ckd', score_full * last_full, query_full), jnp.einsum('cqk,cqd->ckd', probs_full * last_full, grad_full)], axis=-1)
    return (d_queries, grad_prev, grad_cur)

def reference(tokens, cotangent, encoded, w_query, w_key, w_value, w_out, neigh_owner, neigh_row):
    blocks = (neigh_owner * NB_OWN + neigh_row).astype(jnp.int32)
    flat_enc = encoded.reshape(NBLK * NLEN, D)
    flat_enc_full = flat_enc.astype(jnp.float32)
    positions = (jnp.arange(TOKENS, dtype=jnp.int32) % SEQ_LEN).reshape(GROUPS, GROUP)
    last_row = jnp.arange(GROUP, dtype=jnp.int32) == GROUP - 1
    live_mask = (last_row[None, :] | (positions >= GROUP)).astype(jnp.float32)
    live_flat = live_mask.reshape(TOKENS)

    def one_head(head):
        start = (head * HEAD_DIM).astype(jnp.int32)
        wq_head = lax.dynamic_slice_in_dim(w_query, start, HEAD_DIM, 1)
        wk_head = lax.dynamic_slice_in_dim(w_key, start, HEAD_DIM, 1)
        wv_head = lax.dynamic_slice_in_dim(w_value, start, HEAD_DIM, 1)
        wo_head = lax.dynamic_slice_in_dim(w_out, start, HEAD_DIM, 0)
        queries = jnp.dot(tokens, wq_head, preferred_element_type=jnp.float32).astype(jnp.bfloat16)
        w_pair = jnp.concatenate([wk_head, wv_head], axis=1)
        kv_all = jnp.dot(flat_enc, w_pair, preferred_element_type=jnp.float32).astype(jnp.bfloat16)
        kv_all = kv_all.reshape(NBLK, NLEN, 2 * HEAD_DIM)
        kv_group = kv_all[blocks].reshape(GROUPS, NEIGH * NLEN, 2 * HEAD_DIM)
        kv_prev = jnp.concatenate([jnp.zeros_like(kv_group[:1]), kv_group[:-1]], axis=0)
        query_groups = queries.reshape(GROUPS, GROUP, HEAD_DIM)
        attn, attn_probs, probs_half = attend(query_groups, kv_prev, kv_group, last_row, live_mask)
        attn_flat = attn.reshape(TOKENS, HEAD_DIM)
        d_attn = lax.dot_general(cotangent, wo_head, (((1,), (1,)), ((), ())), preferred_element_type=jnp.float32)
        d_attn = (d_attn * live_flat[:, None]).astype(jnp.bfloat16).reshape(GROUPS, GROUP, HEAD_DIM)
        d_queries, grad_prev, grad_cur = attend_back(query_groups, kv_prev, kv_group, last_row, attn_probs, probs_half, d_attn)
        d_kv = grad_cur + jnp.concatenate([grad_prev[1:], jnp.zeros_like(grad_prev[:1])], axis=0)
        per_block = jax.ops.segment_sum(d_kv.reshape(GROUPS * NEIGH, NLEN * 2 * HEAD_DIM), blocks.reshape(-1), NBLK)
        grad_pair = lax.dot_general(flat_enc_full, per_block.reshape(NBLK * NLEN, 2 * HEAD_DIM), (((0,), (0,)), ((), ())), precision=lax.Precision.HIGHEST, preferred_element_type=jnp.float32)
        dq_flat = d_queries.reshape(TOKENS, HEAD_DIM)
        grad_q = lax.dot_general(tokens, dq_flat, (((0,), (0,)), ((), ())), preferred_element_type=jnp.float32)
        grad_o = lax.dot_general(attn_flat, cotangent, (((0,), (0,)), ((), ())), preferred_element_type=jnp.float32)
        return (attn_flat, dq_flat, grad_q, grad_pair, grad_o)
    attn_all, dq_all, grad_q, grad_pair, grad_o = lax.map(one_head, jnp.arange(HEADS, dtype=jnp.int32))
    attn_all = jnp.moveaxis(attn_all, 0, 1).reshape(TOKENS, HD)
    dq_all = jnp.moveaxis(dq_all, 0, 1).reshape(TOKENS, HD)
    block_out = (tokens.astype(jnp.float32) + jnp.dot(attn_all, w_out, preferred_element_type=jnp.float32)).astype(jnp.bfloat16)
    back_sum = lax.dot_general(dq_all, w_query, (((1,), (1,)), ((), ())), preferred_element_type=jnp.float32)
    grad_tokens = (cotangent.astype(jnp.float32) + back_sum).astype(jnp.bfloat16)
    grad_query = jnp.moveaxis(grad_q, 0, 1).reshape(D, HD).astype(jnp.bfloat16)
    grad_key = jnp.moveaxis(grad_pair[:, :, :HEAD_DIM], 0, 1).reshape(D, HD).astype(jnp.bfloat16)
    grad_value = jnp.moveaxis(grad_pair[:, :, HEAD_DIM:], 0, 1).reshape(D, HD).astype(jnp.bfloat16)
    grad_out = grad_o.reshape(HD, D).astype(jnp.bfloat16)
    return (block_out, grad_tokens, grad_query, grad_key, grad_value, grad_out)
```

```python
import math

import jax
import jax.numpy as jnp
from jax import lax
from jax.experimental import pallas as pl
from jax.experimental.pallas import tpu as pltpu
from jax.sharding import PartitionSpec as P

MESH = pl.DeviceIdType.MESH
BF = jnp.bfloat16
F32 = jnp.float32
D = 4096
HALF = D // 2
HEAD = 128
GROUP = 64
NSEQ = 8
RING = 4
TILE = D // NSEQ
MESSAGES = 188
SCALE = 1.0 / math.sqrt(HEAD)
NT = (((1,), (1,)), ((), ()))


def mm(a, b):
    return jnp.dot(a, b, preferred_element_type=F32)


def mm_t(a, b):
    return lax.dot_general(a, b, NT, preferred_element_type=F32)


class Link:
    def __init__(self, send, recv):
        self.send, self.recv, self.sent = send, recv, []

    def message(self, src, dst, peer, land):
        index = len(self.sent)
        out = pltpu.make_async_remote_copy(
            src_ref=src, dst_ref=dst, send_sem=self.send.at[index], recv_sem=self.recv.at[index],
            device_id=peer, device_id_type=MESH)
        back = pltpu.make_async_remote_copy(
            src_ref=land, dst_ref=land, send_sem=self.send.at[index], recv_sem=self.recv.at[index],
            device_id=peer, device_id_type=MESH)
        made = Message(out, back)
        self.sent.append(made)
        return made


class Message:
    def __init__(self, out, back):
        self.out, self.back = out, back

    def start(self):
        self.out.start()

    def wait(self):
        self.back.wait_recv()


class Gather:
    def __init__(self, link, axis, me, at, own=None):
        right, left, far = (me + 1) % RING, (me + 3) % RING, (me + 2) % RING
        own = own or (lambda h: at(me, h))
        to_r, to_l = {axis: right}, {axis: left}
        self.r = [link.message(own(h), at(me, h), to_r, at(left, h)) for h in (0, 1)]
        self.l = [link.message(own(h), at(me, h), to_l, at(right, h)) for h in (0, 1)]
        self.fr = link.message(at(left, 0), at(left, 0), to_r, at(far, 0))
        self.fl = link.message(at(right, 1), at(right, 1), to_l, at(far, 1))

    def start(self):
        self.r[0].start()
        self.l[1].start()
        self.r[1].start()
        self.l[0].start()

    def forward(self):
        self.r[0].wait()
        self.fr.start()
        self.l[1].wait()
        self.fl.start()

    def near(self):
        self.r[1].wait()
        self.l[0].wait()

    def far(self):
        self.fr.wait()
        self.fl.wait()


class Reduce:
    def __init__(self, link, axis, me, part, buf):
        right, left, far = (me + 1) % RING, (me + 3) % RING, (me + 2) % RING
        to_r, to_l = {axis: right}, {axis: left}
        self.me, self.right, self.left, self.part, self.buf = me, right, left, part, buf
        self.r2 = link.message(part(far, 0), buf(0), to_r, buf(0))
        self.r1b = link.message(part(right, 0), buf(1), to_r, buf(1))
        self.r1a = link.message(part(right, 1), buf(2), to_r, buf(2))
        self.l2 = link.message(part(far, 1), buf(3), to_l, buf(3))
        self.l1b = link.message(part(left, 1), buf(4), to_l, buf(4))
        self.l1a = link.message(part(left, 0), buf(5), to_l, buf(5))

    def start_far(self):
        self.r2.start()
        self.l2.start()

    def start_right(self):
        self.r1a.start()

    def start_left(self):
        self.l1a.start()

    def add(self, ref, *bufs):
        total = ref[...].astype(F32)
        for index in bufs:
            total = total + self.buf(index)[...].astype(F32)
        ref[...] = total.astype(BF)

    def middle(self):
        self.r2.wait()
        self.add(self.part(self.right, 0), 0)
        self.r1b.start()
        self.l2.wait()
        self.add(self.part(self.left, 1), 3)
        self.l1b.start()

    def arrive(self):
        self.r1a.wait()
        self.l1a.wait()
        self.r1b.wait()
        self.l1b.wait()

    def total(self, h):
        first, second = ((1, 5), (2, 4))[h]
        total = self.part(self.me, h)[...].astype(F32)
        return total + self.buf(first)[...].astype(F32) + self.buf(second)[...].astype(F32)

    def finish(self):
        self.arrive()
        for h in (0, 1):
            self.part(self.me, h)[...] = self.total(h).astype(BF)


def kernel(
    tok_h, cot_h, enc_h, wq_h, wk_h, wv_h, wo_h, owner, row_of,
    bo, gt, gq, gk, gv, go,
    enc, tok, cot, wq, wkv, wo, own_kv, kv_s, kv_r, qd, stats, ret_s, ret_r,
    fwd, bwd, rx, grad, core_in, rz, dkv_t, plan_row, plan_win, plan_use, slots,
    send, recv, local,
):
    S, X, Y = lax.axis_index("seq"), lax.axis_index("enc"), lax.axis_index("dp")
    Z, C = S // 2, S % 2
    other = Z * 2 + 1 - C
    link = Link(send, recv)

    copies = []

    def fetch(src, dst):
        copy = pltpu.make_async_copy(src, dst, local.at[len(copies)])
        copies.append(copy)
        copy.start()
        return copy

    barrier = pltpu.get_barrier_semaphore()
    peers = [{"enc": (X + 1) % RING}, {"enc": (X + 3) % RING}, {"dp": (Y + 1) % RING}, {"dp": (Y + 3) % RING}]
    peers += [{"seq": (S + d) % NSEQ} for d in range(1, NSEQ)]
    for peer in peers:
        pl.semaphore_signal(barrier, inc=1, device_id=peer, device_id_type=MESH)

    w_copies = [fetch(wk_h, wkv.at[:, pl.ds(0, HEAD)]), fetch(wv_h, wkv.at[:, pl.ds(HEAD, HEAD)])]
    e_copies = [fetch(enc_h.at[pl.ds(2 * c, 2)], enc.at[pl.ds(2 * c, 2)]) for c in range(8)]
    p_copies = [fetch(tok_h, tok.at[X, Y]), fetch(cot_h, cot.at[X, Y]), fetch(wq_h, wq), fetch(wo_h, wo)]

    pl.semaphore_wait(barrier, len(peers))

    def cols(h):
        return pl.ds(h * HALF, HALF)

    xr, xl, xo = (X + 1) % RING, (X + 3) % RING, (X + 2) % RING
    yr, yl, yo = (Y + 1) % RING, (Y + 3) % RING, (Y + 2) % RING
    t_own = lambda h: tok_h.at[:, cols(h)]
    c_own = lambda h: cot_h.at[:, cols(h)]
    tx = Gather(link, "enc", X, lambda p, h: tok.at[p, Y, :, cols(h)], t_own)
    cy = Gather(link, "dp", Y, lambda p, h: cot.at[X, p, :, cols(h)], c_own)
    ty = [
        Gather(link, "dp", Y, lambda p, h, b=b: tok.at[b, p, :, cols(h)], t_own if n == 0 else None)
        for n, b in enumerate((X, xl, xr, xo))
    ]
    cx = [
        Gather(link, "enc", X, lambda p, h, b=b: cot.at[p, b, :, cols(h)], c_own if n == 0 else None)
        for n, b in enumerate((Y, yl, yr, yo))
    ]
    tx.start()
    cy.start()
    ty[0].start()
    cx[0].start()

    def plan(d, carry):
        r = (S + d) % NSEQ
        count = jnp.int32(0)
        rows, wins, uses = [jnp.int32(0)] * 2, [jnp.int32(0)] * 2, [jnp.int32(0)] * 2
        for i in range(4):
            for j in range(2):
                hit = owner[4 * r + i, j] == S
                row = row_of[4 * r + i, j]
                for k in range(2):
                    here = jnp.logical_and(hit, count == k)
                    rows[k] = jnp.where(here, row, rows[k])
                    wins[k] = jnp.where(here, i, wins[k])
                    uses[k] = jnp.where(here, 1, uses[k])
                count = count + jnp.where(hit, 1, 0)
        for k in range(2):
            plan_row[2 * d + k] = rows[k]
            plan_win[2 * d + k] = wins[k]
            plan_use[2 * d + k] = uses[k]
        return carry

    lax.fori_loop(0, NSEQ, plan, 0)
    mine = []
    for i in range(4):
        for j in range(2):
            who = owner[4 * S + i, j]
            rank = jnp.int32(0)
            for before in mine:
                rank = rank + jnp.where(before == who, 1, 0)
            slots[2 * i + j] = who * 2 + rank
            mine.append(who)

    def project(c):
        e_copies[c].wait()
        total = None
        for k in range(4):
            part = mm(enc[2 * c:2 * c + 2, :, k * 1024:(k + 1) * 1024].reshape(256, 1024), wkv[k * 1024:(k + 1) * 1024, :])
            total = part if total is None else total + part
        own_kv[2 * c:2 * c + 2] = total.astype(BF).reshape(2, 128, 256)

    for copy in w_copies:
        copy.wait()
    project(0)
    tx.forward()
    cy.forward()
    project(1)
    tx.near()
    ty[1].start()
    ty[2].start()
    cy.near()
    cx[1].start()
    cx[2].start()
    project(2)
    ty[0].forward()
    cx[0].forward()
    project(3)
    tx.far()
    ty[3].start()
    cy.far()
    cx[3].start()
    project(4)
    project(5)
    ty[1].forward()
    cx[1].forward()
    project(6)
    project(7)
    kv_messages = []
    for d in range(1, NSEQ):
        for k in range(2):
            kv_s[2 * d + k] = own_kv[plan_row[2 * d + k]]
        message = link.message(
            kv_s.at[pl.ds(2 * d, 2)], kv_r.at[pl.ds(2 * S, 2)], {"seq": (S + d) % NSEQ},
            kv_r.at[pl.ds(2 * ((S + NSEQ - d) % NSEQ), 2)])
        message.start()
        kv_messages.append(message)
    for k in range(2):
        kv_r[2 * S + k] = own_kv[plan_row[k]]
    ty[2].forward()
    cx[2].forward()
    ty[3].forward()
    cx[3].forward()
    for copy in p_copies:
        copy.wait()
    for n in range(4):
        ty[n].near()
        cx[n].near()
        if n:
            ty[n - 1].far()
            cx[n - 1].far()
    ty[3].far()
    cx[3].far()

    q, da = None, None
    for k in range(4):
        ks = slice(k * 1024, (k + 1) * 1024)
        part = mm(tok[:, :, :, ks].reshape(256, 1024), wq[ks, :])
        q = part if q is None else q + part
        part = mm_t(cot[:, :, :, ks].reshape(256, 1024), wo[:, ks])
        da = part if da is None else da + part
    token = lax.broadcasted_iota(jnp.int32, (256, HEAD), 0)
    da = jnp.where(jnp.logical_or(token >= GROUP - 1, S > 0), da, 0.0)
    both = pltpu.roll(jnp.concatenate([q, da], axis=1), 1, 0).astype(BF)
    qd[pl.ds(4 * S, 4)] = both.reshape(4, GROUP, 256)

    def zb(p, h):
        return qd.at[pl.ds(4 * (2 * p + C) + 2 * h, 2)]

    def zo(p, h):
        return qd.at[pl.ds(4 * (2 * p + 1 - C) + 2 * h, 2)]

    zr, zl, zf = (Z + 1) % RING, (Z + 3) % RING, (Z + 2) % RING
    sibling = {"seq": other}

    class Column:
        pass

    def seq_peer(p):
        return {"seq": 2 * p + C}

    to_r, to_l = seq_peer(zr), seq_peer(zl)
    qg = Column()
    qg.r = [link.message(zb(Z, h), zb(Z, h), to_r, zb(zl, h)) for h in (0, 1)]
    qg.l = [link.message(zb(Z, h), zb(Z, h), to_l, zb(zr, h)) for h in (0, 1)]
    qg.fr = link.message(zb(zl, 0), zb(zl, 0), to_r, zb(zf, 0))
    qg.fl = link.message(zb(zr, 1), zb(zr, 1), to_l, zb(zf, 1))
    qs = {
        (p, h): link.message(zb(pos, h), zb(pos, h), sibling, zo(pos, h))
        for p, pos in (("me", Z), ("l", zl), ("r", zr), ("f", zf)) for h in (0, 1)
    }
    qg.l[0].start()
    qg.r[0].start()
    qg.l[1].start()
    qg.r[1].start()
    qs["me", 0].start()
    qs["me", 1].start()

    for message in kv_messages:
        message.wait()

    first_row = lax.broadcasted_iota(jnp.int32, (GROUP, 256), 0) == 0
    lane = lax.broadcasted_iota(jnp.int32, (GROUP, HEAD), 1)

    def window(i, pair):
        qw, dw = pair[:, :HEAD], pair[:, HEAD:]
        kv0, kv1 = kv_r[slots[2 * i]], kv_r[slots[2 * i + 1]]
        keys = jnp.concatenate([kv0[:, :HEAD], kv1[:, :HEAD]], axis=0)
        values = jnp.concatenate([kv0[:, HEAD:], kv1[:, HEAD:]], axis=0)
        scores = mm_t(qw, keys) * SCALE
        peak = jnp.max(scores, axis=-1, keepdims=True)
        expos = jnp.exp(scores - peak)
        norm = jnp.sum(expos, axis=-1, keepdims=True)
        probs = expos / norm
        out = mm(probs.astype(BF), values)
        d_probs = mm_t(dw, values)
        delta = jnp.sum(probs * d_probs, axis=-1, keepdims=True)
        d_scores = (probs * (d_probs - delta) * SCALE).astype(BF)
        dq = mm(d_scores, keys)
        column = jnp.where(lane == 0, peak + jnp.log(norm), delta)
        stats[4 * S + i] = jnp.concatenate([column, column], axis=0).T[:8, :]
        return jnp.concatenate([out, dq], axis=1)

    wins = [window(i, qd[4 * S + i + 1]) for i in range(3)]

    qg.l[0].wait()
    qg.r[0].wait()
    qg.fr.start()
    qs["r", 0].start()
    qg.l[1].wait()
    qg.fl.start()
    qg.r[1].wait()
    qs["r", 1].start()
    qs["l", 0].start()
    qs["l", 1].start()
    qs["me", 0].wait()
    qs["r", 0].wait()

    after = qd[(4 * S + 4) % 32].astype(F32)
    last = window(3, jnp.where(first_row, qd[4 * S].astype(F32), after).astype(BF))
    ret_s[...] = last.astype(BF)
    ret = link.message(ret_s, ret_r, {"seq": (S + 1) % NSEQ}, ret_r)
    ret.start()
    st_messages = []
    for d in range(1, NSEQ):
        message = link.message(
            stats.at[pl.ds(4 * S, 4)], stats.at[pl.ds(4 * S, 4)], {"seq": (S + d) % NSEQ},
            stats.at[pl.ds(4 * ((S + NSEQ - d) % NSEQ), 4)])
        message.start()
        st_messages.append(message)
    qg.fr.wait()
    qs["f", 0].start()
    qg.fl.wait()
    qs["f", 1].start()
    ret.wait()
    head = jnp.where(first_row, last, jnp.where(S > 0, ret_r[...].astype(F32), 0.0))
    done = pltpu.roll(jnp.concatenate([head] + wins, axis=0), 255, 0).astype(BF)
    attn, dq = done[:, :HEAD], done[:, HEAD:]

    for n in range(NSEQ):
        c = slice(n * TILE, (n + 1) * TILE)
        fwd[:, :, :, c] = mm(attn, wo[:, c]).astype(BF).reshape(4, 4, 16, TILE)
    ford = (xo, xr, xl, X)
    bord = (yo, yr, yl, Y)
    f1 = [
        Reduce(link, "dp", Y, lambda p, h, b=b: fwd.at[b, p, :, cols(h)], lambda k, n=n: rx.at[0, n, k])
        for n, b in enumerate(ford)
    ]
    b1 = [
        Reduce(link, "enc", X, lambda p, h, b=b: bwd.at[p, b, :, cols(h)], lambda k, n=n: rx.at[1, n, k])
        for n, b in enumerate(bord)
    ]
    f2 = Reduce(link, "enc", X, lambda p, h: fwd.at[p, Y, :, cols(h)], lambda k: rx.at[0, 4, k])
    b2 = Reduce(link, "dp", Y, lambda p, h: bwd.at[X, p, :, cols(h)], lambda k: rx.at[1, 4, k])

    def start(r):
        r.start_far()
        r.start_right()
        r.start_left()

    for r in f1:
        start(r)
    for n in range(NSEQ):
        c = slice(n * TILE, (n + 1) * TILE)
        bwd[:, :, :, c] = mm_t(dq, wq[c, :]).astype(BF).reshape(4, 4, 16, TILE)
    for r in b1:
        start(r)

    gc = [
        [
            link.message(grad.at[a, 2 * ((Z + w) % RING) + 1 - C], core_in.at[a, (Z + w) % RING], sibling, core_in.at[a, (Z + w) % RING])
            for w in (2, 1, 3, 0)
        ]
        for a in range(4)
    ]

    def zpart(a):
        return lambda p, h: grad.at[a, 2 * p + C, pl.ds(64 * h, 64), :]

    class ZReduce(Reduce):
        def __init__(self, a):
            part, buf = zpart(a), lambda k: rz.at[a, k]
            self.me, self.right, self.left, self.part, self.buf = Z, zr, zl, part, buf
            self.r2 = link.message(part(zf, 0), buf(0), to_r, buf(0))
            self.r1b = link.message(part(zr, 0), buf(1), to_r, buf(1))
            self.r1a = link.message(part(zr, 1), buf(2), to_r, buf(2))
            self.l2 = link.message(part(zf, 1), buf(3), to_l, buf(3))
            self.l1b = link.message(part(zl, 1), buf(4), to_l, buf(4))
            self.l1a = link.message(part(zl, 0), buf(5), to_l, buf(5))

    gz = [ZReduce(a) for a in range(4)]

    def core_sum(a, n):
        gc[a][n].wait()
        p = (Z + (2, 1, 3, 0)[n]) % RING
        total = grad[a, 2 * p + C].astype(F32) + core_in[a, p].astype(F32)
        grad[a, 2 * p + C] = total.astype(BF)
        if n == 0:
            gz[a].start_far()
        elif n == 1:
            gz[a].start_right()
        elif n == 2:
            gz[a].start_left()

    dq_t = dq.astype(F32).T.astype(BF)
    attn_t = attn.astype(F32).T.astype(BF)
    for n in range(NSEQ):
        c = slice(n * TILE, (n + 1) * TILE)
        grad[0, n] = mm(dq_t, tok[:, :, :, c].reshape(256, TILE)).astype(BF)
        grad[3, n] = mm(attn_t, cot[:, :, :, c].reshape(256, TILE)).astype(BF)
    for a in (0, 3):
        for n in range(4):
            gc[a][n].start()

    f1[0].middle()
    b1[0].middle()

    for p in "lf":
        for h in (0, 1):
            qs[p, h].wait()
    qs["me", 1].wait()
    qs["r", 1].wait()
    for message in st_messages:
        message.wait()

    def slot(d, k):
        index = 2 * d + k
        r = (S + d) % NSEQ
        b, i, use = plan_row[index], plan_win[index], plan_use[index]
        ahead = qd[(4 * r + i + 1) % 32].astype(F32)
        pair = jnp.where(jnp.logical_and(first_row, i == 3), qd[4 * r].astype(F32), ahead).astype(BF)
        qw, dw = pair[:, :HEAD], pair[:, HEAD:]
        kv = own_kv[b]
        stat = stats[4 * r + i]
        scores = mm_t(kv[:, :HEAD], qw) * SCALE
        probs = jnp.where(use > 0, jnp.exp(scores - stat[0:1, :GROUP]), 0.0)
        d_probs = mm_t(kv[:, HEAD:], dw)
        d_scores = probs * (d_probs - stat[1:2, :GROUP]) * SCALE
        d_keys = mm(d_scores.astype(BF), qw)
        d_values = mm(probs.astype(BF), dw)
        return jnp.concatenate([d_keys, d_values], axis=1).T.astype(BF)

    def slot_pair(d, carry):
        dkv_t[d] = jnp.concatenate([slot(d, 0), slot(d, 1)], axis=1)
        return carry

    lax.fori_loop(0, NSEQ, slot_pair, 0)
    f1[1].middle()
    b1[1].middle()

    def kv_tile(n):
        c = pl.ds(pl.multiple_of(n * TILE, TILE), TILE)
        total = None
        for d in range(NSEQ):
            rows = jnp.concatenate([enc[plan_row[2 * d], :, c], enc[plan_row[2 * d + 1], :, c]], axis=0)
            part = mm(dkv_t[d], rows)
            total = part if total is None else total + part
        total = total.astype(BF)
        grad[1, n] = total[:HEAD]
        grad[2, n] = total[HEAD:]

    for n, w in enumerate((2, 1, 3, 0)):
        kv_tile(2 * ((Z + w) % RING) + 1 - C)
        gc[1][n].start()
        gc[2][n].start()
        if n == 0:
            f1[2].middle()
            b1[2].middle()
        if n == 1:
            f1[3].middle()
            b1[3].middle()
        core_sum(0, n)
        core_sum(3, n)
    f1[0].finish()
    f2.start_far()
    b1[0].finish()
    b2.start_far()
    for n, w in enumerate((2, 1, 3, 0)):
        kv_tile(2 * ((Z + w) % RING) + C)
        core_sum(1, n)
        core_sum(2, n)
        if n == 0:
            gz[0].middle()
            gz[3].middle()
        if n == 1:
            f1[1].finish()
            f2.start_right()
            b1[1].finish()
            b2.start_right()
    f1[2].finish()
    f2.start_left()
    b1[2].finish()
    b2.start_left()
    f2.middle()
    b2.middle()
    gz[1].middle()
    gz[2].middle()
    f1[3].finish()
    b1[3].finish()

    gz[0].arrive()
    for h in (0, 1):
        gq[:, 64 * h:64 * h + 64] = gz[0].total(h).T.astype(BF)
    gz[3].arrive()
    for h in (0, 1):
        go[64 * h:64 * h + 64, :] = gz[3].total(h).astype(BF)
    f2.arrive()
    b2.arrive()
    for h in (0, 1):
        c = slice(h * HALF, (h + 1) * HALF)
        bo[:, c] = (tok[X, Y, :, c].astype(F32) + f2.total(h)).astype(BF)
        gt[:, c] = (cot[X, Y, :, c].astype(F32) + b2.total(h)).astype(BF)
    for a, ref in ((1, gk), (2, gv)):
        gz[a].arrive()
        for h in (0, 1):
            ref[:, 64 * h:64 * h + 64] = gz[a].total(h).T.astype(BF)
    for message in link.sent:
        message.out.wait_send()


def shards(tokens, cotangent, encoded, w_query, w_key, w_value, w_out, neigh_owner, neigh_row):
    any_ref = pl.BlockSpec(memory_space=pl.ANY)
    smem = pl.BlockSpec(memory_space=pltpu.SMEM)
    vmem = pl.BlockSpec(memory_space=pltpu.VMEM)
    shape = jax.ShapeDtypeStruct
    return pl.pallas_call(
        kernel,
        out_shape=(
            shape((16, D), BF), shape((16, D), BF), shape((TILE, HEAD), BF),
            shape((TILE, HEAD), BF), shape((TILE, HEAD), BF), shape((HEAD, TILE), BF),
        ),
        in_specs=[any_ref] * 7 + [smem] * 2,
        out_specs=(vmem,) * 6,
        scratch_shapes=[
            pltpu.VMEM((16, 128, D), BF),
            pltpu.VMEM((4, 4, 16, D), BF),
            pltpu.VMEM((4, 4, 16, D), BF),
            pltpu.VMEM((D, HEAD), BF),
            pltpu.VMEM((D, 2 * HEAD), BF),
            pltpu.VMEM((HEAD, D), BF),
            pltpu.VMEM((16, 128, 256), BF),
            pltpu.VMEM((16, 128, 256), BF),
            pltpu.VMEM((16, 128, 256), BF),
            pltpu.VMEM((32, GROUP, 256), BF),
            pltpu.VMEM((32, 8, 128), F32),
            pltpu.VMEM((GROUP, 256), BF),
            pltpu.VMEM((GROUP, 256), BF),
            pltpu.VMEM((4, 4, 16, D), BF),
            pltpu.VMEM((4, 4, 16, D), BF),
            pltpu.VMEM((2, 5, 6, 16, HALF), BF),
            pltpu.VMEM((4, NSEQ, HEAD, TILE), BF),
            pltpu.VMEM((4, 4, HEAD, TILE), BF),
            pltpu.VMEM((4, 6, 64, TILE), BF),
            pltpu.VMEM((NSEQ, 256, 256), BF),
            pltpu.SMEM((16,), jnp.int32),
            pltpu.SMEM((16,), jnp.int32),
            pltpu.SMEM((16,), jnp.int32),
            pltpu.SMEM((8,), jnp.int32),
            pltpu.SemaphoreType.DMA((MESSAGES + 8,)),
            pltpu.SemaphoreType.DMA((MESSAGES + 8,)),
            pltpu.SemaphoreType.DMA((16,)),
        ],
        compiler_params=pltpu.CompilerParams(
            collective_id=0, has_side_effects=True, vmem_limit_bytes=60 * 1024 * 1024
        ),
        cost_estimate=pl.CostEstimate(flops=10_500_000_000, bytes_accessed=22_000_000, transcendentals=400_000),
    )(tokens, cotangent, encoded, w_query, w_key, w_value, w_out, neigh_owner, neigh_row)


def solution(mesh):
    placed = (
        P(("seq", "enc", "dp"), None),
        P(("seq", "enc", "dp"), None),
        P("seq", None, None),
        P(None, ("enc", "dp")),
        P(None, ("enc", "dp")),
        P(None, ("enc", "dp")),
        P(("enc", "dp"), None),
        P(),
        P(),
    )
    return jax.shard_map(
        shards,
        mesh=mesh,
        in_specs=placed,
        out_specs=(
            P(("seq", "enc", "dp"), None),
            P(("seq", "enc", "dp"), None),
            P("seq", ("enc", "dp")),
            P("seq", ("enc", "dp")),
            P("seq", ("enc", "dp")),
            P(("enc", "dp"), "seq"),
        ),
        check_vma=False,
    )
```

```python
import math

import jax
import jax.numpy as jnp
from jax import lax
from jax.experimental import pallas as pl
from jax.experimental.pallas import tpu as pltpu
from jax.sharding import PartitionSpec as P

MESH = pl.DeviceIdType.MESH
BF = jnp.bfloat16
F32 = jnp.float32
D = 4096
HALF = D // 2
HEAD = 128
GROUP = 64
NSEQ = 8
RING = 4
TILE = D // NSEQ
MESSAGES = 188
SCALE = 1.0 / math.sqrt(HEAD)
NT = (((1,), (1,)), ((), ()))


def mm(a, b):
    return jnp.dot(a, b, preferred_element_type=F32)


def mm_t(a, b):
    return lax.dot_general(a, b, NT, preferred_element_type=F32)


class Link:
    def __init__(self, send, recv):
        self.send, self.recv, self.sent = send, recv, []

    def message(self, src, dst, peer, land):
        index = len(self.sent)
        out = pltpu.make_async_remote_copy(
            src_ref=src, dst_ref=dst, send_sem=self.send.at[index], recv_sem=self.recv.at[index],
            device_id=peer, device_id_type=MESH)
        back = pltpu.make_async_remote_copy(
            src_ref=land, dst_ref=land, send_sem=self.send.at[index], recv_sem=self.recv.at[index],
            device_id=peer, device_id_type=MESH)
        made = Message(out, back)
        self.sent.append(made)
        return made


class Message:
    def __init__(self, out, back):
        self.out, self.back = out, back

    def start(self):
        self.out.start()

    def wait(self):
        self.back.wait_recv()


class Gather:
    def __init__(self, link, axis, me, at, own=None):
        right, left, far = (me + 1) % RING, (me + 3) % RING, (me + 2) % RING
        own = own or (lambda h: at(me, h))
        to_r, to_l = {axis: right}, {axis: left}
        self.r = [link.message(own(h), at(me, h), to_r, at(left, h)) for h in (0, 1)]
        self.l = [link.message(own(h), at(me, h), to_l, at(right, h)) for h in (0, 1)]
        self.fr = link.message(at(left, 0), at(left, 0), to_r, at(far, 0))
        self.fl = link.message(at(right, 1), at(right, 1), to_l, at(far, 1))

    def start(self):
        self.r[0].start()
        self.l[1].start()
        self.r[1].start()
        self.l[0].start()

    def forward(self):
        self.r[0].wait()
        self.fr.start()
        self.l[1].wait()
        self.fl.start()

    def near(self):
        self.r[1].wait()
        self.l[0].wait()

    def far(self):
        self.fr.wait()
        self.fl.wait()


class Reduce:
    def __init__(self, link, axis, me, part, buf):
        right, left, far = (me + 1) % RING, (me + 3) % RING, (me + 2) % RING
        to_r, to_l = {axis: right}, {axis: left}
        self.me, self.right, self.left, self.part, self.buf = me, right, left, part, buf
        self.r2 = link.message(part(far, 0), buf(0), to_r, buf(0))
        self.r1b = link.message(part(right, 0), buf(1), to_r, buf(1))
        self.r1a = link.message(part(right, 1), buf(2), to_r, buf(2))
        self.l2 = link.message(part(far, 1), buf(3), to_l, buf(3))
        self.l1b = link.message(part(left, 1), buf(4), to_l, buf(4))
        self.l1a = link.message(part(left, 0), buf(5), to_l, buf(5))

    def start_far(self):
        self.r2.start()
        self.l2.start()

    def start_right(self):
        self.r1a.start()

    def start_left(self):
        self.l1a.start()

    def add(self, ref, *bufs):
        total = ref[...].astype(F32)
        for index in bufs:
            total = total + self.buf(index)[...].astype(F32)
        ref[...] = total.astype(BF)

    def middle(self):
        self.r2.wait()
        self.add(self.part(self.right, 0), 0)
        self.r1b.start()
        self.l2.wait()
        self.add(self.part(self.left, 1), 3)
        self.l1b.start()

    def arrive(self):
        self.r1a.wait()
        self.l1a.wait()
        self.r1b.wait()
        self.l1b.wait()

    def total(self, h):
        first, second = ((1, 5), (2, 4))[h]
        total = self.part(self.me, h)[...].astype(F32)
        return total + self.buf(first)[...].astype(F32) + self.buf(second)[...].astype(F32)

    def finish(self):
        self.arrive()
        for h in (0, 1):
            self.part(self.me, h)[...] = self.total(h).astype(BF)


def kernel(
    tok_h, cot_h, enc_h, wq_h, wk_h, wv_h, wo_h, owner, row_of,
    bo, gt, gq, gk, gv, go,
    enc, tok, cot, wq, wkv, wo, own_kv, kv_s, kv_r, qd, stats, prev_s, prev_r,
    fwd, bwd, rx, grad, core_in, rz, dkv_t, plan_row, plan_win, plan_use, slots,
    send, recv, local,
):
    S, X, Y = lax.axis_index("seq"), lax.axis_index("enc"), lax.axis_index("dp")
    Z, C = S // 2, S % 2
    other = Z * 2 + 1 - C
    link = Link(send, recv)

    copies = []

    def fetch(src, dst):
        copy = pltpu.make_async_copy(src, dst, local.at[len(copies)])
        copies.append(copy)
        copy.start()
        return copy

    barrier = pltpu.get_barrier_semaphore()
    peers = [{"enc": (X + 1) % RING}, {"enc": (X + 3) % RING}, {"dp": (Y + 1) % RING}, {"dp": (Y + 3) % RING}]
    peers += [{"seq": (S + d) % NSEQ} for d in range(1, NSEQ)]
    for peer in peers:
        pl.semaphore_signal(barrier, inc=1, device_id=peer, device_id_type=MESH)

    w_copies = [fetch(wk_h, wkv.at[:, pl.ds(0, HEAD)]), fetch(wv_h, wkv.at[:, pl.ds(HEAD, HEAD)])]
    e_copies = [fetch(enc_h.at[pl.ds(2 * c, 2)], enc.at[pl.ds(2 * c, 2)]) for c in range(8)]
    p_copies = [fetch(tok_h, tok.at[X, Y]), fetch(cot_h, cot.at[X, Y]), fetch(wq_h, wq), fetch(wo_h, wo)]

    def plan(d, carry):
        r = (S + d) % NSEQ
        count = jnp.int32(0)
        rows, wins, uses = [jnp.int32(0)] * 2, [jnp.int32(0)] * 2, [jnp.int32(0)] * 2
        for i in range(4):
            for j in range(2):
                hit = owner[j, 4 * r + i] == S
                row = row_of[j, 4 * r + i]
                for k in range(2):
                    here = jnp.logical_and(hit, count == k)
                    rows[k] = jnp.where(here, row, rows[k])
                    wins[k] = jnp.where(here, i, wins[k])
                    uses[k] = jnp.where(here, 1, uses[k])
                count = count + jnp.where(hit, 1, 0)
        for k in range(2):
            plan_row[2 * d + k] = rows[k]
            plan_win[2 * d + k] = wins[k]
            plan_use[2 * d + k] = uses[k]
        return carry

    lax.fori_loop(0, NSEQ, plan, 0)
    mine = []
    for i in range(4):
        for j in range(2):
            who = owner[j, 4 * S + i]
            rank = jnp.int32(0)
            for before in mine:
                rank = rank + jnp.where(before == who, 1, 0)
            slots[2 * i + j] = who * 2 + rank
            mine.append(who)

    def project(c):
        e_copies[c].wait()
        total = None
        for k in range(4):
            part = mm(enc[2 * c:2 * c + 2, :, k * 1024:(k + 1) * 1024].reshape(256, 1024), wkv[k * 1024:(k + 1) * 1024, :])
            total = part if total is None else total + part
        own_kv[2 * c:2 * c + 2] = total.astype(BF).reshape(2, 128, 256)

    for copy in w_copies:
        copy.wait()
    pl.semaphore_wait(barrier, len(peers))

    def cols(h):
        return pl.ds(h * HALF, HALF)

    xr, xl, xo = (X + 1) % RING, (X + 3) % RING, (X + 2) % RING
    yr, yl, yo = (Y + 1) % RING, (Y + 3) % RING, (Y + 2) % RING
    t_own = lambda h: tok_h.at[:, cols(h)]
    c_own = lambda h: cot_h.at[:, cols(h)]
    tx = Gather(link, "enc", X, lambda p, h: tok.at[p, Y, :, cols(h)], t_own)
    cy = Gather(link, "dp", Y, lambda p, h: cot.at[X, p, :, cols(h)], c_own)
    ty = [
        Gather(link, "dp", Y, lambda p, h, b=b: tok.at[b, p, :, cols(h)], t_own if n == 0 else None)
        for n, b in enumerate((X, xl, xr, xo))
    ]
    cx = [
        Gather(link, "enc", X, lambda p, h, b=b: cot.at[p, b, :, cols(h)], c_own if n == 0 else None)
        for n, b in enumerate((Y, yl, yr, yo))
    ]
    tx.start()
    cy.start()
    ty[0].start()
    cx[0].start()

    project(0)
    project(1)
    project(2)
    project(3)
    tx.forward()
    cy.forward()
    project(4)
    tx.near()
    ty[1].start()
    ty[2].start()
    cy.near()
    cx[1].start()
    cx[2].start()
    project(5)
    project(6)
    ty[0].forward()
    cx[0].forward()
    project(7)
    kv_messages = []
    for d in range(1, NSEQ):
        for k in range(2):
            kv_s[2 * d + k] = own_kv[plan_row[2 * d + k]]
        message = link.message(
            kv_s.at[pl.ds(2 * d, 2)], kv_r.at[pl.ds(2 * S, 2)], {"seq": (S + d) % NSEQ},
            kv_r.at[pl.ds(2 * ((S + NSEQ - d) % NSEQ), 2)])
        message.start()
        kv_messages.append(message)
    for k in range(2):
        kv_r[2 * S + k] = own_kv[plan_row[k]]
    tx.far()
    ty[3].start()
    cy.far()
    cx[3].start()
    for n in (1, 2):
        ty[n].forward()
        cx[n].forward()
    for copy in p_copies:
        copy.wait()
    ty[3].forward()
    cx[3].forward()
    for message in kv_messages:
        message.wait()
    for j in range(2):
        prev_s[j] = kv_r[slots[6 + j]]
    before = link.message(prev_s, prev_r, {"seq": (S + 1) % NSEQ}, prev_r)
    before.start()
    for n in range(4):
        ty[n].near()
        cx[n].near()
        if n:
            ty[n - 1].far()
            cx[n - 1].far()
    ty[3].far()
    cx[3].far()

    q, da = None, None
    for k in range(4):
        ks = slice(k * 1024, (k + 1) * 1024)
        part = mm(tok[:, :, :, ks].reshape(256, 1024), wq[ks, :])
        q = part if q is None else q + part
        part = mm_t(cot[:, :, :, ks].reshape(256, 1024), wo[:, ks])
        da = part if da is None else da + part
    token = lax.broadcasted_iota(jnp.int32, (256, HEAD), 0)
    da = jnp.where(jnp.logical_or(token >= GROUP - 1, S > 0), da, 0.0)
    both = pltpu.roll(jnp.concatenate([q, da], axis=1), 1, 0).astype(BF)
    qd[pl.ds(4 * S, 4)] = both.reshape(4, GROUP, 256)

    def zb(p, h):
        return qd.at[pl.ds(4 * (2 * p + C) + 2 * h, 2)]

    def zo(p, h):
        return qd.at[pl.ds(4 * (2 * p + 1 - C) + 2 * h, 2)]

    zr, zl, zf = (Z + 1) % RING, (Z + 3) % RING, (Z + 2) % RING
    sibling = {"seq": other}

    class Column:
        pass

    def seq_peer(p):
        return {"seq": 2 * p + C}

    to_r, to_l = seq_peer(zr), seq_peer(zl)
    qg = Column()
    qg.r = [link.message(zb(Z, h), zb(Z, h), to_r, zb(zl, h)) for h in (0, 1)]
    qg.l = [link.message(zb(Z, h), zb(Z, h), to_l, zb(zr, h)) for h in (0, 1)]
    qg.fr = link.message(zb(zl, 0), zb(zl, 0), to_r, zb(zf, 0))
    qg.fl = link.message(zb(zr, 1), zb(zr, 1), to_l, zb(zf, 1))
    qs = {
        (p, h): link.message(zb(pos, h), zb(pos, h), sibling, zo(pos, h))
        for p, pos in (("me", Z), ("l", zl), ("r", zr), ("f", zf)) for h in (0, 1)
    }
    qg.l[0].start()
    qg.r[0].start()
    qg.l[1].start()
    qg.r[1].start()
    qs["me", 0].start()
    qs["me", 1].start()

    first_row = lax.broadcasted_iota(jnp.int32, (GROUP, 256), 0) == 0
    lane = lax.broadcasted_iota(jnp.int32, (GROUP, HEAD), 1)

    def window(block, kv0, kv1):
        pair = qd[4 * S + block]
        qw, dw = pair[:, :HEAD], pair[:, HEAD:]
        keys = jnp.concatenate([kv0[:, :HEAD], kv1[:, :HEAD]], axis=0)
        values = jnp.concatenate([kv0[:, HEAD:], kv1[:, HEAD:]], axis=0)
        scores = mm_t(qw, keys) * SCALE
        peak = jnp.max(scores, axis=-1, keepdims=True)
        expos = jnp.exp(scores - peak)
        norm = jnp.sum(expos, axis=-1, keepdims=True)
        probs = expos / norm
        out = mm(probs.astype(BF), values)
        d_probs = mm_t(dw, values)
        delta = jnp.sum(probs * d_probs, axis=-1, keepdims=True)
        d_scores = (probs * (d_probs - delta) * SCALE).astype(BF)
        dq = mm(d_scores, keys)
        column = jnp.where(lane == 0, peak + jnp.log(norm), delta)
        return jnp.concatenate([out, dq], axis=1), column

    def publish(block, column):
        stats[4 * S + block] = jnp.concatenate([column, column], axis=0).T[:8, :]

    parts = [None] * 4
    for i in range(3):
        parts[i + 1], column = window(i + 1, kv_r[slots[2 * i]], kv_r[slots[2 * i + 1]])
        publish(i + 1, column)
    last, last_column = window(0, kv_r[slots[6]], kv_r[slots[7]])
    before.wait()
    early, early_column = window(0, prev_r[0], prev_r[1])
    parts[0] = jnp.where(first_row, last, jnp.where(S > 0, early, 0.0))
    publish(0, jnp.where(first_row[:, :HEAD], last_column, early_column))
    done = pltpu.roll(jnp.concatenate(parts, axis=0), 255, 0).astype(BF)
    attn, dq = done[:, :HEAD], done[:, HEAD:]
    ford = (xo, xr, xl, X)
    bord = (yo, yr, yl, Y)
    f1 = [
        Reduce(link, "dp", Y, lambda p, h, b=b: fwd.at[b, p, :, cols(h)], lambda k, n=n: rx.at[0, n, k])
        for n, b in enumerate(ford)
    ]
    b1 = [
        Reduce(link, "enc", X, lambda p, h, b=b: bwd.at[p, b, :, cols(h)], lambda k, n=n: rx.at[1, n, k])
        for n, b in enumerate(bord)
    ]
    f2 = Reduce(link, "enc", X, lambda p, h: fwd.at[p, Y, :, cols(h)], lambda k: rx.at[0, 4, k])
    b2 = Reduce(link, "dp", Y, lambda p, h: bwd.at[X, p, :, cols(h)], lambda k: rx.at[1, 4, k])

    st_messages = []

    def stats_and_queries():
        for d in range(1, NSEQ):
            message = link.message(
                stats.at[pl.ds(4 * S, 4)], stats.at[pl.ds(4 * S, 4)], {"seq": (S + d) % NSEQ},
                stats.at[pl.ds(4 * ((S + NSEQ - d) % NSEQ), 4)])
            message.start()
            st_messages.append(message)

    def head_sum(ref, rings, h, tile):
        for n in range(4 * h, 4 * h + 4):
            c = slice(n * TILE, (n + 1) * TILE)
            ref[:, :, :, c] = tile(c).astype(BF).reshape(4, 4, 16, TILE)
        for r in rings:
            (r.l2 if h else r.r2).start()
            (r.r1a if h else r.l1a).start()

    stats_and_queries()
    for h in (0, 1):
        head_sum(fwd, f1, h, lambda c: mm(attn, wo[:, c]))
        head_sum(bwd, b1, h, lambda c: mm_t(dq, wq[c, :]))
        if h == 0:
            qg.l[0].wait()
            qs["r", 0].start()
            qg.r[0].wait()
            qg.fr.start()
            qg.l[1].wait()
            qg.fl.start()
            qg.r[1].wait()
            qs["r", 1].start()
            qs["l", 0].start()
            qs["l", 1].start()

    gc = [
        [
            link.message(grad.at[a, 2 * ((Z + w) % RING) + 1 - C], core_in.at[a, (Z + w) % RING], sibling, core_in.at[a, (Z + w) % RING])
            for w in (2, 1, 3, 0)
        ]
        for a in range(4)
    ]

    def zpart(a):
        return lambda p, h: grad.at[a, 2 * p + C, pl.ds(64 * h, 64), :]

    class ZReduce(Reduce):
        def __init__(self, a):
            part, buf = zpart(a), lambda k: rz.at[a, k]
            self.me, self.right, self.left, self.part, self.buf = Z, zr, zl, part, buf
            self.r2 = link.message(part(zf, 0), buf(0), to_r, buf(0))
            self.r1b = link.message(part(zr, 0), buf(1), to_r, buf(1))
            self.r1a = link.message(part(zr, 1), buf(2), to_r, buf(2))
            self.l2 = link.message(part(zf, 1), buf(3), to_l, buf(3))
            self.l1b = link.message(part(zl, 1), buf(4), to_l, buf(4))
            self.l1a = link.message(part(zl, 0), buf(5), to_l, buf(5))

    gz = [ZReduce(a) for a in range(4)]

    def core_sum(a, n):
        gc[a][n].wait()
        p = (Z + (2, 1, 3, 0)[n]) % RING
        total = grad[a, 2 * p + C].astype(F32) + core_in[a, p].astype(F32)
        grad[a, 2 * p + C] = total.astype(BF)
        if n == 0:
            gz[a].start_far()
        elif n == 1:
            gz[a].start_right()
        elif n == 2:
            gz[a].start_left()

    def token_gradient(a, left, right):
        left_t = left.astype(F32).T.astype(BF)
        for n in range(NSEQ):
            c = slice(n * TILE, (n + 1) * TILE)
            grad[a, n] = mm(left_t, right[:, :, :, c].reshape(256, TILE)).astype(BF)
        for n in range(4):
            gc[a][n].start()

    token_gradient(3, attn, cot)
    qg.fr.wait()
    qs["f", 0].start()
    qg.fl.wait()
    qs["f", 1].start()
    token_gradient(0, dq, tok)
    f1[0].middle()
    b1[0].middle()
    for n in range(4):
        core_sum(3, n)
    f1[1].middle()
    b1[1].middle()
    for n in range(4):
        core_sum(0, n)
    for message in qs.values():
        message.wait()
    for message in st_messages:
        message.wait()

    first_lane = lax.broadcasted_iota(jnp.int32, (8, HEAD), 1) == 0

    def slot(d, k):
        index = 2 * d + k
        r = (S + d) % NSEQ
        b, i, use = plan_row[index], plan_win[index], plan_use[index]
        ahead = qd[(4 * r + i + 1) % 32].astype(F32)
        pair = jnp.where(jnp.logical_and(first_row, i == 3), qd[4 * r].astype(F32), ahead).astype(BF)
        qw, dw = pair[:, :HEAD], pair[:, HEAD:]
        kv = own_kv[b]
        stat = jnp.where(jnp.logical_and(first_lane, i == 3), stats[4 * r], stats[(4 * r + i + 1) % 32])
        scores = mm_t(kv[:, :HEAD], qw) * SCALE
        probs = jnp.where(use > 0, jnp.exp(scores - stat[0:1, :GROUP]), 0.0)
        d_probs = mm_t(kv[:, HEAD:], dw)
        d_scores = probs * (d_probs - stat[1:2, :GROUP]) * SCALE
        d_keys = mm(d_scores.astype(BF), qw)
        d_values = mm(probs.astype(BF), dw)
        return jnp.concatenate([d_keys, d_values], axis=1).T.astype(BF)

    def slot_pair(d, carry):
        dkv_t[d] = jnp.concatenate([slot(d, 0), slot(d, 1)], axis=1)
        return carry

    lax.fori_loop(0, NSEQ, slot_pair, 0)
    gz[3].middle()
    f1[2].middle()
    b1[2].middle()
    f1[3].middle()
    b1[3].middle()

    def kv_tile(n):
        c = pl.ds(pl.multiple_of(n * TILE, TILE), TILE)
        total = None
        for d in range(NSEQ):
            rows = jnp.concatenate([enc[plan_row[2 * d], :, c], enc[plan_row[2 * d + 1], :, c]], axis=0)
            part = mm(dkv_t[d], rows)
            total = part if total is None else total + part
        total = total.astype(BF)
        grad[1, n] = total[:HEAD]
        grad[2, n] = total[HEAD:]

    for n, w in enumerate((2, 1, 3, 0)):
        kv_tile(2 * ((Z + w) % RING) + 1 - C)
        gc[1][n].start()
        gc[2][n].start()
        kv_tile(2 * ((Z + w) % RING) + C)
        core_sum(1, n)
        core_sum(2, n)
        if n == 0:
            gz[0].middle()
        if n == 2:
            f1[0].finish()
            f2.start_far()
            b1[0].finish()
            b2.start_far()
        if n == 3:
            f1[1].finish()
            f2.start_right()
            b1[1].finish()
            b2.start_right()
    f1[2].finish()
    f2.start_left()
    b1[2].finish()
    b2.start_left()
    f2.middle()
    b2.middle()
    gz[1].middle()
    gz[2].middle()
    f1[3].finish()
    b1[3].finish()

    gz[0].arrive()
    for h in (0, 1):
        gq[:, 64 * h:64 * h + 64] = gz[0].total(h).T.astype(BF)
    gz[3].arrive()
    for h in (0, 1):
        go[64 * h:64 * h + 64, :] = gz[3].total(h).astype(BF)
    f2.arrive()
    b2.arrive()
    for h in (0, 1):
        c = slice(h * HALF, (h + 1) * HALF)
        bo[:, c] = (tok[X, Y, :, c].astype(F32) + f2.total(h)).astype(BF)
        gt[:, c] = (cot[X, Y, :, c].astype(F32) + b2.total(h)).astype(BF)
    for a, ref in ((1, gk), (2, gv)):
        gz[a].arrive()
        for h in (0, 1):
            ref[:, 64 * h:64 * h + 64] = gz[a].total(h).T.astype(BF)
    for message in link.sent:
        message.out.wait_send()


def deliver(*refs):
    inputs, outputs, held, sems = refs[:6], refs[6:12], refs[12:18], refs[18]
    into = [pltpu.make_async_copy(inputs[n], held[n], sems.at[n]) for n in range(6)]
    out = [pltpu.make_async_copy(held[n], outputs[n], sems.at[6 + n]) for n in range(6)]
    for copy in into:
        copy.start()
    for n in range(6):
        into[n].wait()
        out[n].start()
    for copy in out:
        copy.wait()


def shards(tokens, cotangent, encoded, w_query, w_key, w_value, w_out, neigh_owner, neigh_row):
    any_ref = pl.BlockSpec(memory_space=pl.ANY)
    smem = pl.BlockSpec(memory_space=pltpu.SMEM)
    vmem = pl.BlockSpec(memory_space=pltpu.VMEM)
    shape = jax.ShapeDtypeStruct
    results = pl.pallas_call(
        kernel,
        out_shape=(
            shape((16, D), BF), shape((16, D), BF), shape((TILE, HEAD), BF),
            shape((TILE, HEAD), BF), shape((TILE, HEAD), BF), shape((HEAD, TILE), BF),
        ),
        in_specs=[any_ref] * 7 + [smem] * 2,
        out_specs=(vmem,) * 6,
        scratch_shapes=[
            pltpu.VMEM((16, 128, D), BF),
            pltpu.VMEM((4, 4, 16, D), BF),
            pltpu.VMEM((4, 4, 16, D), BF),
            pltpu.VMEM((D, HEAD), BF),
            pltpu.VMEM((D, 2 * HEAD), BF),
            pltpu.VMEM((HEAD, D), BF),
            pltpu.VMEM((16, 128, 256), BF),
            pltpu.VMEM((16, 128, 256), BF),
            pltpu.VMEM((16, 128, 256), BF),
            pltpu.VMEM((32, GROUP, 256), BF),
            pltpu.VMEM((32, 8, 128), F32),
            pltpu.VMEM((2, 128, 256), BF),
            pltpu.VMEM((2, 128, 256), BF),
            pltpu.VMEM((4, 4, 16, D), BF),
            pltpu.VMEM((4, 4, 16, D), BF),
            pltpu.VMEM((2, 5, 6, 16, HALF), BF),
            pltpu.VMEM((4, NSEQ, HEAD, TILE), BF),
            pltpu.VMEM((4, 4, HEAD, TILE), BF),
            pltpu.VMEM((4, 6, 64, TILE), BF),
            pltpu.VMEM((NSEQ, 256, 256), BF),
            pltpu.SMEM((16,), jnp.int32),
            pltpu.SMEM((16,), jnp.int32),
            pltpu.SMEM((16,), jnp.int32),
            pltpu.SMEM((8,), jnp.int32),
            pltpu.SemaphoreType.DMA((MESSAGES + 8,)),
            pltpu.SemaphoreType.DMA((MESSAGES + 8,)),
            pltpu.SemaphoreType.DMA((16,)),
        ],
        compiler_params=pltpu.CompilerParams(
            collective_id=0, has_side_effects=True, vmem_limit_bytes=60 * 1024 * 1024
        ),
        cost_estimate=pl.CostEstimate(flops=10_500_000_000, bytes_accessed=22_000_000, transcendentals=400_000),
    )(tokens, cotangent, encoded, w_query, w_key, w_value, w_out, neigh_owner.T, neigh_row.T)
    return pl.pallas_call(
        deliver,
        out_shape=tuple(shape(r.shape, r.dtype) for r in results),
        in_specs=[any_ref] * 6,
        out_specs=(any_ref,) * 6,
        scratch_shapes=[pltpu.VMEM(r.shape, r.dtype) for r in results] + [pltpu.SemaphoreType.DMA((12,))],
        compiler_params=pltpu.CompilerParams(vmem_limit_bytes=60 * 1024 * 1024),
    )(*results)


def solution(mesh):
    placed = (
        P(("seq", "enc", "dp"), None),
        P(("seq", "enc", "dp"), None),
        P("seq", None, None),
        P(None, ("enc", "dp")),
        P(None, ("enc", "dp")),
        P(None, ("enc", "dp")),
        P(("enc", "dp"), None),
        P(),
        P(),
    )
    return jax.shard_map(
        shards,
        mesh=mesh,
        in_specs=placed,
        out_specs=(
            P(("seq", "enc", "dp"), None),
            P(("seq", "enc", "dp"), None),
            P("seq", ("enc", "dp")),
            P("seq", ("enc", "dp")),
            P("seq", ("enc", "dp")),
            P(("enc", "dp"), "seq"),
        ),
        check_vma=False,
    )
```

```python
import math

import jax
import jax.numpy as jnp
from jax import lax
from jax.experimental import pallas as pl
from jax.experimental.pallas import tpu as pltpu
from jax.sharding import PartitionSpec as P

MESH = pl.DeviceIdType.MESH
BF = jnp.bfloat16
F32 = jnp.float32
D = 4096
HALF = D // 2
HEAD = 128
GROUP = 64
NSEQ = 8
RING = 4
TILE = D // NSEQ
MESSAGES = 188
SCALE = 1.0 / math.sqrt(HEAD)
NT = (((1,), (1,)), ((), ()))


def mm(a, b):
    return jnp.dot(a, b, preferred_element_type=F32)


def mm_t(a, b):
    return lax.dot_general(a, b, NT, preferred_element_type=F32)


class Link:
    def __init__(self, send, recv):
        self.send, self.recv, self.sent = send, recv, []

    def drain(self):
        for message in self.sent:
            if message.pending:
                message.pending = False
                message.out.wait_send()

    def message(self, src, dst, peer, land):
        index = len(self.sent)
        out = pltpu.make_async_remote_copy(
            src_ref=src, dst_ref=dst, send_sem=self.send.at[index], recv_sem=self.recv.at[index],
            device_id=peer, device_id_type=MESH)
        back = pltpu.make_async_remote_copy(
            src_ref=land, dst_ref=land, send_sem=self.send.at[index], recv_sem=self.recv.at[index],
            device_id=peer, device_id_type=MESH)
        made = Message(out, back)
        self.sent.append(made)
        return made


class Message:
    def __init__(self, out, back):
        self.out, self.back = out, back
        self.pending = False

    def start(self):
        self.pending = True
        self.out.start()

    def wait(self):
        self.back.wait_recv()


class Gather:
    def __init__(self, link, axis, me, at, own=None):
        right, left, far = (me + 1) % RING, (me + 3) % RING, (me + 2) % RING
        own = own or (lambda h: at(me, h))
        to_r, to_l = {axis: right}, {axis: left}
        self.r = [link.message(own(h), at(me, h), to_r, at(left, h)) for h in (0, 1)]
        self.l = [link.message(own(h), at(me, h), to_l, at(right, h)) for h in (0, 1)]
        self.fr = link.message(at(left, 0), at(left, 0), to_r, at(far, 0))
        self.fl = link.message(at(right, 1), at(right, 1), to_l, at(far, 1))

    def start(self):
        self.r[0].start()
        self.l[1].start()
        self.r[1].start()
        self.l[0].start()

    def forward(self):
        self.r[0].wait()
        self.fr.start()
        self.l[1].wait()
        self.fl.start()

    def near(self):
        self.r[1].wait()
        self.l[0].wait()

    def far(self):
        self.fr.wait()
        self.fl.wait()


class Reduce:
    def __init__(self, link, axis, me, part, buf):
        right, left, far = (me + 1) % RING, (me + 3) % RING, (me + 2) % RING
        to_r, to_l = {axis: right}, {axis: left}
        self.me, self.right, self.left, self.part, self.buf = me, right, left, part, buf
        self.r2 = link.message(part(far, 0), buf(0), to_r, buf(0))
        self.r1b = link.message(part(right, 0), buf(1), to_r, buf(1))
        self.r1a = link.message(part(right, 1), buf(2), to_r, buf(2))
        self.l2 = link.message(part(far, 1), buf(3), to_l, buf(3))
        self.l1b = link.message(part(left, 1), buf(4), to_l, buf(4))
        self.l1a = link.message(part(left, 0), buf(5), to_l, buf(5))

    def start_far(self):
        self.r2.start()
        self.l2.start()

    def start_right(self):
        self.r1a.start()

    def start_left(self):
        self.l1a.start()

    def add(self, ref, *bufs):
        total = ref[...].astype(F32)
        for index in bufs:
            total = total + self.buf(index)[...].astype(F32)
        ref[...] = total.astype(BF)

    def middle(self):
        self.r2.wait()
        self.add(self.part(self.right, 0), 0)
        self.r1b.start()
        self.l2.wait()
        self.add(self.part(self.left, 1), 3)
        self.l1b.start()

    def arrive(self):
        self.r1a.wait()
        self.l1a.wait()
        self.r1b.wait()
        self.l1b.wait()

    def total(self, h):
        first, second = ((1, 5), (2, 4))[h]
        total = self.part(self.me, h)[...].astype(F32)
        return total + self.buf(first)[...].astype(F32) + self.buf(second)[...].astype(F32)

    def finish(self):
        self.arrive()
        for h in (0, 1):
            self.part(self.me, h)[...] = self.total(h).astype(BF)


def kernel(
    tok_h, cot_h, enc_h, wq_h, wk_h, wv_h, wo_h, owner, row_of,
    bo_h, gt_h, gq_h, gk_h, gv_h, go_h,
    enc, tok, cot, wq, wkv, wo, own_kv, kv_s, kv_r, qd, stats, prev_s, prev_r, q_rows, d_rows,
    fwd, bwd, rx, grad, core_in, rz, dkv_t, plan_row, plan_win, plan_use, slots,
    bo, gt, gq, gk, gv, go, send, recv, local,
):
    S, X, Y = lax.axis_index("seq"), lax.axis_index("enc"), lax.axis_index("dp")
    Z, C = S // 2, S % 2
    other = Z * 2 + 1 - C
    link = Link(send, recv)

    copies = []

    def fetch(src, dst):
        copy = pltpu.make_async_copy(src, dst, local.at[len(copies)])
        copies.append(copy)
        copy.start()
        return copy

    barrier = pltpu.get_barrier_semaphore()
    peers = [{"enc": (X + 1) % RING}, {"enc": (X + 3) % RING}, {"dp": (Y + 1) % RING}, {"dp": (Y + 3) % RING}]
    peers += [{"seq": (S + d) % NSEQ} for d in range(1, NSEQ)]
    for peer in peers:
        pl.semaphore_signal(barrier, inc=1, device_id=peer, device_id_type=MESH)

    w_copies = [fetch(wk_h, wkv.at[:, pl.ds(0, HEAD)]), fetch(wv_h, wkv.at[:, pl.ds(HEAD, HEAD)])]
    e_copies = [fetch(enc_h.at[pl.ds(2 * c, 2)], enc.at[pl.ds(2 * c, 2)]) for c in range(8)]
    p_copies = [fetch(tok_h, tok.at[X, Y]), fetch(cot_h, cot.at[X, Y]), fetch(wq_h, wq), fetch(wo_h, wo)]

    def plan(d, carry):
        r = (S + d) % NSEQ
        count = jnp.int32(0)
        rows, wins, uses = [jnp.int32(0)] * 2, [jnp.int32(0)] * 2, [jnp.int32(0)] * 2
        for i in range(4):
            for j in range(2):
                hit = owner[j, 4 * r + i] == S
                row = row_of[j, 4 * r + i]
                for k in range(2):
                    here = jnp.logical_and(hit, count == k)
                    rows[k] = jnp.where(here, row, rows[k])
                    wins[k] = jnp.where(here, i, wins[k])
                    uses[k] = jnp.where(here, 1, uses[k])
                count = count + jnp.where(hit, 1, 0)
        for k in range(2):
            plan_row[2 * d + k] = rows[k]
            plan_win[2 * d + k] = wins[k]
            plan_use[2 * d + k] = uses[k]
        return carry

    lax.fori_loop(0, NSEQ, plan, 0)
    mine = []
    for i in range(4):
        for j in range(2):
            who = owner[j, 4 * S + i]
            rank = jnp.int32(0)
            for before in mine:
                rank = rank + jnp.where(before == who, 1, 0)
            slots[2 * i + j] = who * 2 + rank
            mine.append(who)

    def project(c):
        e_copies[c].wait()
        total = None
        for k in range(4):
            part = mm(enc[2 * c:2 * c + 2, :, k * 1024:(k + 1) * 1024].reshape(256, 1024), wkv[k * 1024:(k + 1) * 1024, :])
            total = part if total is None else total + part
        own_kv[2 * c:2 * c + 2] = total.astype(BF).reshape(2, 128, 256)

    for copy in w_copies:
        copy.wait()
    pl.semaphore_wait(barrier, len(peers))

    def cols(h):
        return pl.ds(h * HALF, HALF)

    xr, xl, xo = (X + 1) % RING, (X + 3) % RING, (X + 2) % RING
    yr, yl, yo = (Y + 1) % RING, (Y + 3) % RING, (Y + 2) % RING
    t_own = lambda h: tok_h.at[:, cols(h)]
    c_own = lambda h: cot_h.at[:, cols(h)]
    tx = Gather(link, "enc", X, lambda p, h: tok.at[p, Y, :, cols(h)], t_own)
    cy = Gather(link, "dp", Y, lambda p, h: cot.at[X, p, :, cols(h)], c_own)
    ty = [
        Gather(link, "dp", Y, lambda p, h, b=b: tok.at[b, p, :, cols(h)], t_own if n == 0 else None)
        for n, b in enumerate((X, xl, xr, xo))
    ]
    cx = [
        Gather(link, "enc", X, lambda p, h, b=b: cot.at[p, b, :, cols(h)], c_own if n == 0 else None)
        for n, b in enumerate((Y, yl, yr, yo))
    ]
    tx.start()
    cy.start()
    ty[0].start()
    cx[0].start()

    project(0)
    project(1)
    project(2)
    project(3)
    tx.forward()
    cy.forward()
    project(4)
    tx.near()
    ty[1].start()
    ty[2].start()
    cy.near()
    cx[1].start()
    cx[2].start()
    project(5)
    project(6)
    ty[0].forward()
    cx[0].forward()
    project(7)
    kv_messages = []
    for d in range(1, NSEQ):
        for k in range(2):
            kv_s[2 * d + k] = own_kv[plan_row[2 * d + k]]
        message = link.message(
            kv_s.at[pl.ds(2 * d, 2)], kv_r.at[pl.ds(2 * S, 2)], {"seq": (S + d) % NSEQ},
            kv_r.at[pl.ds(2 * ((S + NSEQ - d) % NSEQ), 2)])
        message.start()
        kv_messages.append(message)
    for k in range(2):
        kv_r[2 * S + k] = own_kv[plan_row[k]]
    tx.far()
    ty[3].start()
    cy.far()
    cx[3].start()
    for n in (1, 2):
        ty[n].forward()
        cx[n].forward()
    for copy in p_copies:
        copy.wait()
    ty[3].forward()
    cx[3].forward()
    for message in kv_messages:
        message.wait()
    for j in range(2):
        prev_s[j] = kv_r[slots[6 + j]]
    before = link.message(prev_s, prev_r, {"seq": (S + 1) % NSEQ}, prev_r)
    before.start()
    for n in range(4):
        ty[n].near()
        cx[n].near()
        if n:
            ty[n - 1].far()
            cx[n - 1].far()

    def project_rows(xs, ys):
        q, da = None, None
        for k in range(4):
            ks = slice(k * 1024, (k + 1) * 1024)
            rows = jnp.concatenate([tok[b, :, :, ks].reshape(GROUP, 1024) for b in xs], axis=0)
            part = mm(rows, wq[ks, :])
            q = part if q is None else q + part
            rows = jnp.concatenate([cot[:, b, :, ks].reshape(GROUP, 1024) for b in ys], axis=0)
            part = mm_t(rows, wo[:, ks])
            da = part if da is None else da + part
        for n, b in enumerate(xs):
            q_rows[b] = q[GROUP * n:GROUP * (n + 1)].reshape(4, 16, HEAD)
        for n, b in enumerate(ys):
            d_rows[:, b] = da[GROUP * n:GROUP * (n + 1)].reshape(4, 16, HEAD)

    project_rows((X, xl, xr), (Y, yl, yr))
    ty[3].far()
    cx[3].far()

    project_rows((xo,), (yo,))
    q, da = q_rows[...].reshape(256, HEAD), d_rows[...].reshape(256, HEAD)
    token = lax.broadcasted_iota(jnp.int32, (256, HEAD), 0)
    da = jnp.where(jnp.logical_or(token >= GROUP - 1, S > 0), da, 0.0)
    both = pltpu.roll(jnp.concatenate([q, da], axis=1), 1, 0).astype(BF)
    qd[pl.ds(4 * S, 4)] = both.reshape(4, GROUP, 256)

    def zb(p, h):
        return qd.at[pl.ds(4 * (2 * p + C) + 2 * h, 2)]

    def zo(p, h):
        return qd.at[pl.ds(4 * (2 * p + 1 - C) + 2 * h, 2)]

    zr, zl, zf = (Z + 1) % RING, (Z + 3) % RING, (Z + 2) % RING
    sibling = {"seq": other}

    class Column:
        pass

    def seq_peer(p):
        return {"seq": 2 * p + C}

    to_r, to_l = seq_peer(zr), seq_peer(zl)
    qg = Column()
    qg.r = [link.message(zb(Z, h), zb(Z, h), to_r, zb(zl, h)) for h in (0, 1)]
    qg.l = [link.message(zb(Z, h), zb(Z, h), to_l, zb(zr, h)) for h in (0, 1)]
    qg.fr = link.message(zb(zl, 0), zb(zl, 0), to_r, zb(zf, 0))
    qg.fl = link.message(zb(zr, 1), zb(zr, 1), to_l, zb(zf, 1))
    qs = {
        (p, h): link.message(zb(pos, h), zb(pos, h), sibling, zo(pos, h))
        for p, pos in (("me", Z), ("l", zl), ("r", zr), ("f", zf)) for h in (0, 1)
    }
    qg.l[0].start()
    qg.r[0].start()
    qg.l[1].start()
    qg.r[1].start()
    qs["me", 0].start()
    qs["me", 1].start()

    first_row = lax.broadcasted_iota(jnp.int32, (GROUP, 256), 0) == 0
    lane = lax.broadcasted_iota(jnp.int32, (GROUP, HEAD), 1)

    def window(block, kv0, kv1):
        pair = qd[4 * S + block]
        qw, dw = pair[:, :HEAD], pair[:, HEAD:]
        keys = jnp.concatenate([kv0[:, :HEAD], kv1[:, :HEAD]], axis=0)
        values = jnp.concatenate([kv0[:, HEAD:], kv1[:, HEAD:]], axis=0)
        scores = mm_t(qw, keys) * SCALE
        peak = jnp.max(scores, axis=-1, keepdims=True)
        expos = jnp.exp(scores - peak)
        norm = jnp.sum(expos, axis=-1, keepdims=True)
        probs = expos / norm
        out = mm(probs.astype(BF), values)
        d_probs = mm_t(dw, values)
        delta = jnp.sum(probs * d_probs, axis=-1, keepdims=True)
        d_scores = (probs * (d_probs - delta) * SCALE).astype(BF)
        dq = mm(d_scores, keys)
        column = jnp.where(lane == 0, peak + jnp.log(norm), delta)
        return jnp.concatenate([out, dq], axis=1), column

    def publish(block, column):
        stats[4 * S + block] = jnp.concatenate([column, column], axis=0).T[:8, :]

    parts = [None] * 4
    for i in range(3):
        parts[i + 1], column = window(i + 1, kv_r[slots[2 * i]], kv_r[slots[2 * i + 1]])
        publish(i + 1, column)
    last, last_column = window(0, kv_r[slots[6]], kv_r[slots[7]])
    before.wait()
    early, early_column = window(0, prev_r[0], prev_r[1])
    parts[0] = jnp.where(first_row, last, jnp.where(S > 0, early, 0.0))
    publish(0, jnp.where(first_row[:, :HEAD], last_column, early_column))
    done = pltpu.roll(jnp.concatenate(parts, axis=0), 255, 0).astype(BF)
    attn, dq = done[:, :HEAD], done[:, HEAD:]
    ford = (xo, xr, xl, X)
    bord = (yo, yr, yl, Y)
    f1 = [
        Reduce(link, "dp", Y, lambda p, h, b=b: fwd.at[b, p, :, cols(h)], lambda k, n=n: rx.at[0, n, k])
        for n, b in enumerate(ford)
    ]
    b1 = [
        Reduce(link, "enc", X, lambda p, h, b=b: bwd.at[p, b, :, cols(h)], lambda k, n=n: rx.at[1, n, k])
        for n, b in enumerate(bord)
    ]
    f2 = Reduce(link, "enc", X, lambda p, h: fwd.at[p, Y, :, cols(h)], lambda k: rx.at[0, 4, k])
    b2 = Reduce(link, "dp", Y, lambda p, h: bwd.at[X, p, :, cols(h)], lambda k: rx.at[1, 4, k])

    st_messages = []

    def stats_and_queries():
        for d in range(1, NSEQ):
            message = link.message(
                stats.at[pl.ds(4 * S, 4)], stats.at[pl.ds(4 * S, 4)], {"seq": (S + d) % NSEQ},
                stats.at[pl.ds(4 * ((S + NSEQ - d) % NSEQ), 4)])
            message.start()
            st_messages.append(message)

    def head_sum(ref, rings, h, tile):
        for n in range(4 * h, 4 * h + 4):
            c = slice(n * TILE, (n + 1) * TILE)
            ref[:, :, :, c] = tile(c).astype(BF).reshape(4, 4, 16, TILE)
        for r in rings:
            (r.l2 if h else r.r2).start()
        for r in rings[:1]:
            (r.r1a if h else r.l1a).start()

    stats_and_queries()
    for h in (0, 1):
        head_sum(fwd, f1, h, lambda c: mm(attn, wo[:, c]))
        head_sum(bwd, b1, h, lambda c: mm_t(dq, wq[c, :]))
        if h == 0:
            qg.l[0].wait()
            qs["r", 0].start()
            qg.r[0].wait()
            qg.fr.start()
            qg.l[1].wait()
            qg.fl.start()
            qg.r[1].wait()
            qs["r", 1].start()
            qs["l", 0].start()
            qs["l", 1].start()

    early = [m for m in link.sent if m.pending and m not in [r.r2 for r in f1 + b1] + [r.l2 for r in f1 + b1] + [r.r1a for r in f1 + b1] + [r.l1a for r in f1 + b1]]

    gc = [
        [
            link.message(grad.at[a, 2 * ((Z + w) % RING) + 1 - C], core_in.at[a, (Z + w) % RING], sibling, core_in.at[a, (Z + w) % RING])
            for w in (2, 1, 3, 0)
        ]
        for a in range(4)
    ]

    def zpart(a):
        return lambda p, h: grad.at[a, 2 * p + C, pl.ds(64 * h, 64), :]

    class ZReduce(Reduce):
        def __init__(self, a):
            part, buf = zpart(a), lambda k: rz.at[a, k]
            self.me, self.right, self.left, self.part, self.buf = Z, zr, zl, part, buf
            self.r2 = link.message(part(zf, 0), buf(0), to_r, buf(0))
            self.r1b = link.message(part(zr, 0), buf(1), to_r, buf(1))
            self.r1a = link.message(part(zr, 1), buf(2), to_r, buf(2))
            self.l2 = link.message(part(zf, 1), buf(3), to_l, buf(3))
            self.l1b = link.message(part(zl, 1), buf(4), to_l, buf(4))
            self.l1a = link.message(part(zl, 0), buf(5), to_l, buf(5))

    gz = [ZReduce(a) for a in range(4)]

    def core_sum(a, n):
        gc[a][n].wait()
        p = (Z + (2, 1, 3, 0)[n]) % RING
        total = grad[a, 2 * p + C].astype(F32) + core_in[a, p].astype(F32)
        grad[a, 2 * p + C] = total.astype(BF)
        if n == 0:
            gz[a].start_far()
        elif n == 1:
            gz[a].start_right()
        elif n == 2:
            gz[a].start_left()

    def token_gradient(a, left, right):
        left_t = left.astype(F32).T.astype(BF)
        for n in range(NSEQ):
            c = slice(n * TILE, (n + 1) * TILE)
            grad[a, n] = mm(left_t, right[:, :, :, c].reshape(256, TILE)).astype(BF)
        for n in range(4):
            gc[a][n].start()

    token_gradient(3, attn, cot)
    qg.fr.wait()
    qs["f", 0].start()
    qg.fl.wait()
    qs["f", 1].start()
    token_gradient(0, dq, tok)
    f1[0].middle()
    b1[0].middle()
    for r in (f1[1], b1[1], f1[2], b1[2], f1[3], b1[3]):
        r.start_right()
        r.start_left()
    for n in range(4):
        core_sum(3, n)
    f1[1].middle()
    b1[1].middle()
    for n in range(4):
        core_sum(0, n)
    for message in qs.values():
        message.wait()
    for message in st_messages:
        message.wait()

    first_lane = lax.broadcasted_iota(jnp.int32, (8, HEAD), 1) == 0

    def slot(d, k):
        index = 2 * d + k
        r = (S + d) % NSEQ
        b, i, use = plan_row[index], plan_win[index], plan_use[index]
        ahead = qd[(4 * r + i + 1) % 32].astype(F32)
        pair = jnp.where(jnp.logical_and(first_row, i == 3), qd[4 * r].astype(F32), ahead).astype(BF)
        qw, dw = pair[:, :HEAD], pair[:, HEAD:]
        kv = own_kv[b]
        stat = jnp.where(jnp.logical_and(first_lane, i == 3), stats[4 * r], stats[(4 * r + i + 1) % 32])
        scores = mm_t(kv[:, :HEAD], qw) * SCALE
        probs = jnp.where(use > 0, jnp.exp(scores - stat[0:1, :GROUP]), 0.0)
        d_probs = mm_t(kv[:, HEAD:], dw)
        d_scores = probs * (d_probs - stat[1:2, :GROUP]) * SCALE
        d_keys = mm(d_scores.astype(BF), qw)
        d_values = mm(probs.astype(BF), dw)
        return jnp.concatenate([d_keys, d_values], axis=1).T.astype(BF)

    def slot_pair(d, carry):
        dkv_t[d] = jnp.concatenate([slot(d, 0), slot(d, 1)], axis=1)
        return carry

    lax.fori_loop(0, NSEQ, slot_pair, 0)
    gz[3].middle()
    f1[2].middle()
    b1[2].middle()

    def kv_tile(n):
        c = pl.ds(pl.multiple_of(n * TILE, TILE), TILE)
        total = None
        for d in range(NSEQ):
            rows = jnp.concatenate([enc[plan_row[2 * d], :, c], enc[plan_row[2 * d + 1], :, c]], axis=0)
            part = mm(dkv_t[d], rows)
            total = part if total is None else total + part
        total = total.astype(BF)
        grad[1, n] = total[:HEAD]
        grad[2, n] = total[HEAD:]

    for n, w in enumerate((2, 1, 3, 0)):
        kv_tile(2 * ((Z + w) % RING) + 1 - C)
        gc[1][n].start()
        gc[2][n].start()
        kv_tile(2 * ((Z + w) % RING) + C)
        core_sum(1, n)
        core_sum(2, n)
        if n == 0:
            gz[0].middle()
        if n == 2:
            f1[0].finish()
            f2.start_far()
            b1[0].finish()
            b2.start_far()
            f1[3].middle()
            b1[3].middle()
        if n == 3:
            f1[1].finish()
            f2.start_right()
            b1[1].finish()
            b2.start_right()
    f1[2].finish()
    f2.start_left()
    b1[2].finish()
    b2.start_left()
    for message in early:
        message.pending = False
        message.out.wait_send()
    f2.middle()
    b2.middle()
    gz[1].middle()
    gz[2].middle()
    f1[3].finish()
    b1[3].finish()

    gz[0].arrive()
    for h in (0, 1):
        gq[:, 64 * h:64 * h + 64] = gz[0].total(h).T.astype(BF)
    fetch(gq, gq_h)
    gz[3].arrive()
    for h in (0, 1):
        go[64 * h:64 * h + 64, :] = gz[3].total(h).astype(BF)
    fetch(go, go_h)
    f2.arrive()
    b2.arrive()
    for h in (0, 1):
        c = slice(h * HALF, (h + 1) * HALF)
        bo[:, c] = (tok[X, Y, :, c].astype(F32) + f2.total(h)).astype(BF)
        gt[:, c] = (cot[X, Y, :, c].astype(F32) + b2.total(h)).astype(BF)
    fetch(bo, bo_h)
    fetch(gt, gt_h)
    for a, ref, whole in ((1, gk, gk_h), (2, gv, gv_h)):
        gz[a].arrive()
        for h in (0, 1):
            ref[:, 64 * h:64 * h + 64] = gz[a].total(h).T.astype(BF)
        fetch(ref, whole)
    link.drain()
    for copy in copies[14:]:
        copy.wait()


def deliver(*refs):
    inputs, outputs, held, sems = refs[:6], refs[6:12], refs[12:18], refs[18]
    into = [pltpu.make_async_copy(inputs[n], held[n], sems.at[n]) for n in range(6)]
    out = [pltpu.make_async_copy(held[n], outputs[n], sems.at[6 + n]) for n in range(6)]
    for copy in into:
        copy.start()
    for n in range(6):
        into[n].wait()
        out[n].start()
    for copy in out:
        copy.wait()


def shards(tokens, cotangent, encoded, w_query, w_key, w_value, w_out, neigh_owner, neigh_row):
    any_ref = pl.BlockSpec(memory_space=pl.ANY)
    smem = pl.BlockSpec(memory_space=pltpu.SMEM)
    shape = jax.ShapeDtypeStruct
    results = pl.pallas_call(
        kernel,
        out_shape=(
            shape((16, D), BF), shape((16, D), BF), shape((TILE, HEAD), BF),
            shape((TILE, HEAD), BF), shape((TILE, HEAD), BF), shape((HEAD, TILE), BF),
        ),
        in_specs=[any_ref] * 7 + [smem] * 2,
        out_specs=(any_ref,) * 6,
        scratch_shapes=[
            pltpu.VMEM((16, 128, D), BF),
            pltpu.VMEM((4, 4, 16, D), BF),
            pltpu.VMEM((4, 4, 16, D), BF),
            pltpu.VMEM((D, HEAD), BF),
            pltpu.VMEM((D, 2 * HEAD), BF),
            pltpu.VMEM((HEAD, D), BF),
            pltpu.VMEM((16, 128, 256), BF),
            pltpu.VMEM((16, 128, 256), BF),
            pltpu.VMEM((16, 128, 256), BF),
            pltpu.VMEM((32, GROUP, 256), BF),
            pltpu.VMEM((32, 8, 128), F32),
            pltpu.VMEM((2, 128, 256), BF),
            pltpu.VMEM((2, 128, 256), BF),
            pltpu.VMEM((4, 4, 16, HEAD), F32),
            pltpu.VMEM((4, 4, 16, HEAD), F32),
            pltpu.VMEM((4, 4, 16, D), BF),
            pltpu.VMEM((4, 4, 16, D), BF),
            pltpu.VMEM((2, 5, 6, 16, HALF), BF),
            pltpu.VMEM((4, NSEQ, HEAD, TILE), BF),
            pltpu.VMEM((4, 4, HEAD, TILE), BF),
            pltpu.VMEM((4, 6, 64, TILE), BF),
            pltpu.VMEM((NSEQ, 256, 256), BF),
            pltpu.SMEM((16,), jnp.int32),
            pltpu.SMEM((16,), jnp.int32),
            pltpu.SMEM((16,), jnp.int32),
            pltpu.SMEM((8,), jnp.int32),
            pltpu.VMEM((16, D), BF),
            pltpu.VMEM((16, D), BF),
            pltpu.VMEM((TILE, HEAD), BF),
            pltpu.VMEM((TILE, HEAD), BF),
            pltpu.VMEM((TILE, HEAD), BF),
            pltpu.VMEM((HEAD, TILE), BF),
            pltpu.SemaphoreType.DMA((MESSAGES + 8,)),
            pltpu.SemaphoreType.DMA((MESSAGES + 8,)),
            pltpu.SemaphoreType.DMA((24,)),
        ],
        compiler_params=pltpu.CompilerParams(
            collective_id=0, has_side_effects=True, vmem_limit_bytes=60 * 1024 * 1024
        ),
        cost_estimate=pl.CostEstimate(flops=10_500_000_000, bytes_accessed=22_000_000, transcendentals=400_000),
    )(tokens, cotangent, encoded, w_query, w_key, w_value, w_out, neigh_owner.T, neigh_row.T)
    return pl.pallas_call(
        deliver,
        out_shape=tuple(shape(r.shape, r.dtype) for r in results),
        in_specs=[any_ref] * 6,
        out_specs=(any_ref,) * 6,
        scratch_shapes=[pltpu.VMEM(r.shape, r.dtype) for r in results] + [pltpu.SemaphoreType.DMA((12,))],
        compiler_params=pltpu.CompilerParams(vmem_limit_bytes=60 * 1024 * 1024),
    )(*results)


def solution(mesh):
    placed = (
        P(("seq", "enc", "dp"), None),
        P(("seq", "enc", "dp"), None),
        P("seq", None, None),
        P(None, ("enc", "dp")),
        P(None, ("enc", "dp")),
        P(None, ("enc", "dp")),
        P(("enc", "dp"), None),
        P(),
        P(),
    )
    return jax.shard_map(
        shards,
        mesh=mesh,
        in_specs=placed,
        out_specs=(
            P(("seq", "enc", "dp"), None),
            P(("seq", "enc", "dp"), None),
            P("seq", ("enc", "dp")),
            P("seq", ("enc", "dp")),
            P("seq", ("enc", "dp")),
            P(("enc", "dp"), "seq"),
        ),
        check_vma=False,
    )
```

```python
import math

import jax
import jax.numpy as jnp
from jax import lax
from jax.experimental import pallas as pl
from jax.experimental.pallas import tpu as pltpu
from jax.sharding import PartitionSpec as P

MESH = pl.DeviceIdType.MESH
BF = jnp.bfloat16
F32 = jnp.float32
D = 4096
HALF = D // 2
HEAD = 128
GROUP = 64
NSEQ = 8
RING = 4
TILE = D // NSEQ
MESSAGES = 188
SCALE = 1.0 / math.sqrt(HEAD)
NT = (((1,), (1,)), ((), ()))


def mm(a, b):
    return jnp.dot(a, b, preferred_element_type=F32)


def mm_t(a, b):
    return lax.dot_general(a, b, NT, preferred_element_type=F32)


class Link:
    def __init__(self, send, recv):
        self.send, self.recv, self.sent = send, recv, []

    def drain(self):
        for message in self.sent:
            if message.pending:
                message.pending = False
                message.out.wait_send()

    def message(self, src, dst, peer, land):
        index = len(self.sent)
        out = pltpu.make_async_remote_copy(
            src_ref=src, dst_ref=dst, send_sem=self.send.at[index], recv_sem=self.recv.at[index],
            device_id=peer, device_id_type=MESH)
        back = pltpu.make_async_remote_copy(
            src_ref=land, dst_ref=land, send_sem=self.send.at[index], recv_sem=self.recv.at[index],
            device_id=peer, device_id_type=MESH)
        made = Message(out, back)
        self.sent.append(made)
        return made


class Message:
    def __init__(self, out, back):
        self.out, self.back = out, back
        self.pending = False

    def start(self):
        self.pending = True
        self.out.start()

    def wait(self):
        self.back.wait_recv()


class Gather:
    def __init__(self, link, axis, me, at, own=None):
        right, left, far = (me + 1) % RING, (me + 3) % RING, (me + 2) % RING
        own = own or (lambda h: at(me, h))
        to_r, to_l = {axis: right}, {axis: left}
        self.r = [link.message(own(h), at(me, h), to_r, at(left, h)) for h in (0, 1)]
        self.l = [link.message(own(h), at(me, h), to_l, at(right, h)) for h in (0, 1)]
        self.fr = link.message(at(left, 0), at(left, 0), to_r, at(far, 0))
        self.fl = link.message(at(right, 1), at(right, 1), to_l, at(far, 1))

    def start(self):
        self.r[0].start()
        self.l[1].start()
        self.r[1].start()
        self.l[0].start()

    def forward(self):
        self.r[0].wait()
        self.fr.start()
        self.l[1].wait()
        self.fl.start()

    def near(self):
        self.r[1].wait()
        self.l[0].wait()

    def far(self):
        self.fr.wait()
        self.fl.wait()


class Reduce:
    def __init__(self, link, axis, me, part, buf):
        right, left, far = (me + 1) % RING, (me + 3) % RING, (me + 2) % RING
        to_r, to_l = {axis: right}, {axis: left}
        self.me, self.right, self.left, self.part, self.buf = me, right, left, part, buf
        self.r2 = link.message(part(far, 0), buf(0), to_r, buf(0))
        self.r1b = link.message(part(right, 0), buf(1), to_r, buf(1))
        self.r1a = link.message(part(right, 1), buf(2), to_r, buf(2))
        self.l2 = link.message(part(far, 1), buf(3), to_l, buf(3))
        self.l1b = link.message(part(left, 1), buf(4), to_l, buf(4))
        self.l1a = link.message(part(left, 0), buf(5), to_l, buf(5))

    def start_far(self):
        self.r2.start()
        self.l2.start()

    def start_right(self):
        self.r1a.start()

    def start_left(self):
        self.l1a.start()

    def add(self, ref, *bufs):
        total = ref[...].astype(F32)
        for index in bufs:
            total = total + self.buf(index)[...].astype(F32)
        ref[...] = total.astype(BF)

    def middle(self):
        self.r2.wait()
        self.add(self.part(self.right, 0), 0)
        self.r1b.start()
        self.l2.wait()
        self.add(self.part(self.left, 1), 3)
        self.l1b.start()

    def arrive(self):
        self.r1a.wait()
        self.l1a.wait()
        self.r1b.wait()
        self.l1b.wait()

    def total(self, h):
        first, second = ((1, 5), (2, 4))[h]
        total = self.part(self.me, h)[...].astype(F32)
        return total + self.buf(first)[...].astype(F32) + self.buf(second)[...].astype(F32)

    def finish(self):
        self.arrive()
        for h in (0, 1):
            self.part(self.me, h)[...] = self.total(h).astype(BF)


def kernel(
    tok_h, cot_h, enc_h, wq_h, wk_h, wv_h, wo_h, owner, row_of,
    bo_h, gt_h, gq_h, gk_h, gv_h, go_h,
    enc, tok, cot, wq, wkv, wo, own_kv, kv_s, kv_r, qd, stats, prev_s, prev_r, q_rows, d_rows,
    fwd, bwd, rx, grad, core_in, rz, dkv_t, plan_row, plan_win, plan_use, slots,
    bo, gt, gq, gk, gv, go, send, recv, local,
):
    S, X, Y = lax.axis_index("seq"), lax.axis_index("enc"), lax.axis_index("dp")
    Z, C = S // 2, S % 2
    other = Z * 2 + 1 - C
    link = Link(send, recv)

    copies = []

    def fetch(src, dst):
        copy = pltpu.make_async_copy(src, dst, local.at[len(copies)])
        copies.append(copy)
        copy.start()
        return copy

    barrier = pltpu.get_barrier_semaphore()
    peers = [{"enc": (X + 1) % RING}, {"enc": (X + 3) % RING}, {"dp": (Y + 1) % RING}, {"dp": (Y + 3) % RING}]
    peers += [{"seq": (S + d) % NSEQ} for d in range(1, NSEQ)]
    for peer in peers:
        pl.semaphore_signal(barrier, inc=1, device_id=peer, device_id_type=MESH)

    w_copies = [fetch(wk_h, wkv.at[:, pl.ds(0, HEAD)]), fetch(wv_h, wkv.at[:, pl.ds(HEAD, HEAD)])]
    e_copies = [fetch(enc_h.at[pl.ds(2 * c, 2)], enc.at[pl.ds(2 * c, 2)]) for c in range(8)]
    p_copies = [fetch(tok_h, tok.at[X, Y]), fetch(cot_h, cot.at[X, Y]), fetch(wq_h, wq), fetch(wo_h, wo)]

    def plan(d, carry):
        r = (S + d) % NSEQ
        count = jnp.int32(0)
        rows, wins, uses = [jnp.int32(0)] * 2, [jnp.int32(0)] * 2, [jnp.int32(0)] * 2
        for i in range(4):
            for j in range(2):
                hit = owner[j, 4 * r + i] == S
                row = row_of[j, 4 * r + i]
                for k in range(2):
                    here = jnp.logical_and(hit, count == k)
                    rows[k] = jnp.where(here, row, rows[k])
                    wins[k] = jnp.where(here, i, wins[k])
                    uses[k] = jnp.where(here, 1, uses[k])
                count = count + jnp.where(hit, 1, 0)
        for k in range(2):
            plan_row[2 * d + k] = rows[k]
            plan_win[2 * d + k] = wins[k]
            plan_use[2 * d + k] = uses[k]
        return carry

    lax.fori_loop(0, NSEQ, plan, 0)
    mine = []
    for i in range(4):
        for j in range(2):
            who = owner[j, 4 * S + i]
            rank = jnp.int32(0)
            for before in mine:
                rank = rank + jnp.where(before == who, 1, 0)
            slots[2 * i + j] = who * 2 + rank
            mine.append(who)

    def project(c):
        e_copies[c].wait()
        total = None
        for k in range(4):
            part = mm(enc[2 * c:2 * c + 2, :, k * 1024:(k + 1) * 1024].reshape(256, 1024), wkv[k * 1024:(k + 1) * 1024, :])
            total = part if total is None else total + part
        own_kv[2 * c:2 * c + 2] = total.astype(BF).reshape(2, 128, 256)

    for copy in w_copies:
        copy.wait()
    pl.semaphore_wait(barrier, len(peers))

    def cols(h):
        return pl.ds(h * HALF, HALF)

    xr, xl, xo = (X + 1) % RING, (X + 3) % RING, (X + 2) % RING
    yr, yl, yo = (Y + 1) % RING, (Y + 3) % RING, (Y + 2) % RING
    t_own = lambda h: tok_h.at[:, cols(h)]
    c_own = lambda h: cot_h.at[:, cols(h)]
    tx = Gather(link, "enc", X, lambda p, h: tok.at[p, Y, :, cols(h)], t_own)
    cy = Gather(link, "dp", Y, lambda p, h: cot.at[X, p, :, cols(h)], c_own)
    ty = [
        Gather(link, "dp", Y, lambda p, h, b=b: tok.at[b, p, :, cols(h)], t_own if n == 0 else None)
        for n, b in enumerate((X, xl, xr, xo))
    ]
    cx = [
        Gather(link, "enc", X, lambda p, h, b=b: cot.at[p, b, :, cols(h)], c_own if n == 0 else None)
        for n, b in enumerate((Y, yl, yr, yo))
    ]
    tx.start()
    cy.start()
    ty[0].start()
    cx[0].start()

    project(0)
    project(1)
    project(2)
    project(3)
    tx.forward()
    cy.forward()
    project(4)
    tx.near()
    ty[1].start()
    ty[2].start()
    cy.near()
    cx[1].start()
    cx[2].start()
    project(5)
    project(6)
    ty[0].forward()
    cx[0].forward()
    project(7)
    kv_messages = []
    for d in range(1, NSEQ):
        for k in range(2):
            kv_s[2 * d + k] = own_kv[plan_row[2 * d + k]]
        message = link.message(
            kv_s.at[pl.ds(2 * d, 2)], kv_r.at[pl.ds(2 * S, 2)], {"seq": (S + d) % NSEQ},
            kv_r.at[pl.ds(2 * ((S + NSEQ - d) % NSEQ), 2)])
        message.start()
        kv_messages.append(message)
    for k in range(2):
        kv_r[2 * S + k] = own_kv[plan_row[k]]
    tx.far()
    ty[3].start()
    cy.far()
    cx[3].start()
    for n in (1, 2):
        ty[n].forward()
        cx[n].forward()
    for copy in p_copies:
        copy.wait()
    ty[3].forward()
    cx[3].forward()
    for message in kv_messages:
        message.wait()
    for j in range(2):
        prev_s[j] = kv_r[slots[6 + j]]
    before = link.message(prev_s, prev_r, {"seq": (S + 1) % NSEQ}, prev_r)
    before.start()
    for n in range(4):
        ty[n].near()
        cx[n].near()
        if n:
            ty[n - 1].far()
            cx[n - 1].far()

    def project_rows(xs, ys):
        q, da = None, None
        for k in range(4):
            ks = slice(k * 1024, (k + 1) * 1024)
            rows = jnp.concatenate([tok[b, :, :, ks].reshape(GROUP, 1024) for b in xs], axis=0)
            part = mm(rows, wq[ks, :])
            q = part if q is None else q + part
            rows = jnp.concatenate([cot[:, b, :, ks].reshape(GROUP, 1024) for b in ys], axis=0)
            part = mm_t(rows, wo[:, ks])
            da = part if da is None else da + part
        for n, b in enumerate(xs):
            q_rows[b] = q[GROUP * n:GROUP * (n + 1)].reshape(4, 16, HEAD)
        for n, b in enumerate(ys):
            d_rows[:, b] = da[GROUP * n:GROUP * (n + 1)].reshape(4, 16, HEAD)

    project_rows((X, xl, xr), (Y, yl, yr))
    ty[3].far()
    cx[3].far()

    project_rows((xo,), (yo,))
    q, da = q_rows[...].reshape(256, HEAD), d_rows[...].reshape(256, HEAD)
    token = lax.broadcasted_iota(jnp.int32, (256, HEAD), 0)
    da = jnp.where(jnp.logical_or(token >= GROUP - 1, S > 0), da, 0.0)
    both = pltpu.roll(jnp.concatenate([q, da], axis=1), 1, 0).astype(BF)
    qd[pl.ds(4 * S, 4)] = both.reshape(4, GROUP, 256)

    def zb(p, h):
        return qd.at[pl.ds(4 * (2 * p + C) + 2 * h, 2)]

    def zo(p, h):
        return qd.at[pl.ds(4 * (2 * p + 1 - C) + 2 * h, 2)]

    zr, zl, zf = (Z + 1) % RING, (Z + 3) % RING, (Z + 2) % RING
    sibling = {"seq": other}

    class Column:
        pass

    def seq_peer(p):
        return {"seq": 2 * p + C}

    to_r, to_l = seq_peer(zr), seq_peer(zl)
    qg = Column()
    qg.r = [link.message(zb(Z, h), zb(Z, h), to_r, zb(zl, h)) for h in (0, 1)]
    qg.l = [link.message(zb(Z, h), zb(Z, h), to_l, zb(zr, h)) for h in (0, 1)]
    qg.fr = link.message(zb(zl, 0), zb(zl, 0), to_r, zb(zf, 0))
    qg.fl = link.message(zb(zr, 1), zb(zr, 1), to_l, zb(zf, 1))
    qs = {
        (p, h): link.message(zb(pos, h), zb(pos, h), sibling, zo(pos, h))
        for p, pos in (("me", Z), ("l", zl), ("r", zr), ("f", zf)) for h in (0, 1)
    }
    qg.l[0].start()
    qg.r[0].start()
    qg.l[1].start()
    qg.r[1].start()
    qs["me", 0].start()
    qs["me", 1].start()

    first_row = lax.broadcasted_iota(jnp.int32, (GROUP, 256), 0) == 0
    lane = lax.broadcasted_iota(jnp.int32, (GROUP, HEAD), 1)

    def window(block, kv0, kv1):
        pair = qd[4 * S + block]
        qw, dw = pair[:, :HEAD], pair[:, HEAD:]
        keys = jnp.concatenate([kv0[:, :HEAD], kv1[:, :HEAD]], axis=0)
        values = jnp.concatenate([kv0[:, HEAD:], kv1[:, HEAD:]], axis=0)
        scores = mm_t(qw, keys) * SCALE
        peak = jnp.max(scores, axis=-1, keepdims=True)
        expos = jnp.exp(scores - peak)
        norm = jnp.sum(expos, axis=-1, keepdims=True)
        probs = expos / norm
        out = mm(probs.astype(BF), values)
        d_probs = mm_t(dw, values)
        delta = jnp.sum(probs * d_probs, axis=-1, keepdims=True)
        d_scores = (probs * (d_probs - delta) * SCALE).astype(BF)
        dq = mm(d_scores, keys)
        column = jnp.where(lane == 0, peak + jnp.log(norm), delta)
        return jnp.concatenate([out, dq], axis=1), column

    def publish(block, column):
        stats[4 * S + block] = jnp.concatenate([column, column], axis=0).T[:8, :]

    parts = [None] * 4
    for i in range(3):
        parts[i + 1], column = window(i + 1, kv_r[slots[2 * i]], kv_r[slots[2 * i + 1]])
        publish(i + 1, column)
    last, last_column = window(0, kv_r[slots[6]], kv_r[slots[7]])
    before.wait()
    early, early_column = window(0, prev_r[0], prev_r[1])
    parts[0] = jnp.where(first_row, last, jnp.where(S > 0, early, 0.0))
    publish(0, jnp.where(first_row[:, :HEAD], last_column, early_column))
    done = pltpu.roll(jnp.concatenate(parts, axis=0), 255, 0).astype(BF)
    attn, dq = done[:, :HEAD], done[:, HEAD:]
    ford = (xo, xr, xl, X)
    bord = (yo, yr, yl, Y)
    f1 = [
        Reduce(link, "dp", Y, lambda p, h, b=b: fwd.at[b, p, :, cols(h)], lambda k, n=n: rx.at[0, n, k])
        for n, b in enumerate(ford)
    ]
    b1 = [
        Reduce(link, "enc", X, lambda p, h, b=b: bwd.at[p, b, :, cols(h)], lambda k, n=n: rx.at[1, n, k])
        for n, b in enumerate(bord)
    ]
    f2 = Reduce(link, "enc", X, lambda p, h: fwd.at[p, Y, :, cols(h)], lambda k: rx.at[0, 4, k])
    b2 = Reduce(link, "dp", Y, lambda p, h: bwd.at[X, p, :, cols(h)], lambda k: rx.at[1, 4, k])

    st_messages = []

    def stats_and_queries():
        for d in range(1, NSEQ):
            message = link.message(
                stats.at[pl.ds(4 * S, 4)], stats.at[pl.ds(4 * S, 4)], {"seq": (S + d) % NSEQ},
                stats.at[pl.ds(4 * ((S + NSEQ - d) % NSEQ), 4)])
            message.start()
            st_messages.append(message)

    def head_sum(ref, rings, h, tile):
        for n in range(4 * h, 4 * h + 4):
            c = slice(n * TILE, (n + 1) * TILE)
            ref[:, :, :, c] = tile(c).astype(BF).reshape(4, 4, 16, TILE)
        for r in rings:
            (r.l2 if h else r.r2).start()
        for r in rings[:1]:
            (r.r1a if h else r.l1a).start()

    stats_and_queries()
    for h in (0, 1):
        head_sum(fwd, f1, h, lambda c: mm(attn, wo[:, c]))
        head_sum(bwd, b1, h, lambda c: mm_t(dq, wq[c, :]))
        if h == 0:
            qg.l[0].wait()
            qs["r", 0].start()
            qg.r[0].wait()
            qg.fr.start()
            qg.l[1].wait()
            qg.fl.start()
            qg.r[1].wait()
            qs["r", 1].start()
            qs["l", 0].start()
            qs["l", 1].start()

    early = [m for m in link.sent if m.pending and m not in [r.r2 for r in f1 + b1] + [r.l2 for r in f1 + b1] + [r.r1a for r in f1 + b1] + [r.l1a for r in f1 + b1]]

    gc = [
        [
            link.message(grad.at[a, 2 * ((Z + w) % RING) + 1 - C], core_in.at[a, (Z + w) % RING], sibling, core_in.at[a, (Z + w) % RING])
            for w in (2, 1, 3, 0)
        ]
        for a in range(4)
    ]

    def zpart(a):
        return lambda p, h: grad.at[a, 2 * p + C, pl.ds(64 * h, 64), :]

    class ZReduce(Reduce):
        def __init__(self, a):
            part, buf = zpart(a), lambda k: rz.at[a, k]
            self.me, self.right, self.left, self.part, self.buf = Z, zr, zl, part, buf
            self.r2 = link.message(part(zf, 0), buf(0), to_r, buf(0))
            self.r1b = link.message(part(zr, 0), buf(1), to_r, buf(1))
            self.r1a = link.message(part(zr, 1), buf(2), to_r, buf(2))
            self.l2 = link.message(part(zf, 1), buf(3), to_l, buf(3))
            self.l1b = link.message(part(zl, 1), buf(4), to_l, buf(4))
            self.l1a = link.message(part(zl, 0), buf(5), to_l, buf(5))

    gz = [ZReduce(a) for a in range(4)]

    def core_sum(a, n):
        gc[a][n].wait()
        p = (Z + (2, 1, 3, 0)[n]) % RING
        total = grad[a, 2 * p + C].astype(F32) + core_in[a, p].astype(F32)
        grad[a, 2 * p + C] = total.astype(BF)
        if n == 0:
            gz[a].start_far()
        elif n == 1:
            gz[a].start_right()
        elif n == 2:
            gz[a].start_left()

    def token_gradient(a, left, right):
        left_t = left.astype(F32).T.astype(BF)
        for n in range(NSEQ):
            c = slice(n * TILE, (n + 1) * TILE)
            grad[a, n] = mm(left_t, right[:, :, :, c].reshape(256, TILE)).astype(BF)
        for n in range(4):
            gc[a][n].start()

    token_gradient(3, attn, cot)
    qg.fr.wait()
    qs["f", 0].start()
    qg.fl.wait()
    qs["f", 1].start()
    token_gradient(0, dq, tok)
    f1[0].middle()
    b1[0].middle()
    for r in (f1[1], b1[1], f1[2], b1[2], f1[3], b1[3]):
        r.start_right()
        r.start_left()
    for n in range(4):
        core_sum(3, n)
    f1[1].middle()
    b1[1].middle()
    for n in range(4):
        core_sum(0, n)
    for message in qs.values():
        message.wait()
    for message in st_messages:
        message.wait()

    first_lane = lax.broadcasted_iota(jnp.int32, (8, HEAD), 1) == 0

    def slot(d, k):
        index = 2 * d + k
        r = (S + d) % NSEQ
        b, i, use = plan_row[index], plan_win[index], plan_use[index]
        ahead = qd[(4 * r + i + 1) % 32].astype(F32)
        pair = jnp.where(jnp.logical_and(first_row, i == 3), qd[4 * r].astype(F32), ahead).astype(BF)
        qw, dw = pair[:, :HEAD], pair[:, HEAD:]
        kv = own_kv[b]
        stat = jnp.where(jnp.logical_and(first_lane, i == 3), stats[4 * r], stats[(4 * r + i + 1) % 32])
        scores = mm_t(kv[:, :HEAD], qw) * SCALE
        probs = jnp.where(use > 0, jnp.exp(scores - stat[0:1, :GROUP]), 0.0)
        d_probs = mm_t(kv[:, HEAD:], dw)
        d_scores = probs * (d_probs - stat[1:2, :GROUP]) * SCALE
        d_keys = mm(d_scores.astype(BF), qw)
        d_values = mm(probs.astype(BF), dw)
        return jnp.concatenate([d_keys, d_values], axis=1).T.astype(BF)

    def slot_pair(d, carry):
        dkv_t[d] = jnp.concatenate([slot(d, 0), slot(d, 1)], axis=1)
        return carry

    lax.fori_loop(0, NSEQ, slot_pair, 0)
    gz[3].middle()
    f1[2].middle()
    b1[2].middle()

    def kv_tile(n):
        c = pl.ds(pl.multiple_of(n * TILE, TILE), TILE)
        total = None
        for d in range(NSEQ):
            rows = jnp.concatenate([enc[plan_row[2 * d], :, c], enc[plan_row[2 * d + 1], :, c]], axis=0)
            part = mm(dkv_t[d], rows)
            total = part if total is None else total + part
        total = total.astype(BF)
        grad[1, n] = total[:HEAD]
        grad[2, n] = total[HEAD:]

    for n, w in enumerate((2, 1, 3, 0)):
        kv_tile(2 * ((Z + w) % RING) + 1 - C)
        gc[1][n].start()
        gc[2][n].start()
        kv_tile(2 * ((Z + w) % RING) + C)
        core_sum(1, n)
        core_sum(2, n)
        if n == 0:
            gz[0].middle()
        if n == 1:
            f1[0].finish()
            f2.start_far()
            b1[0].finish()
            b2.start_far()
            f1[3].middle()
            b1[3].middle()
        if n == 2:
            f1[1].finish()
            f2.start_right()
            b1[1].finish()
            b2.start_right()
        if n == 3:
            f1[2].finish()
            f2.start_left()
            b1[2].finish()
            b2.start_left()
    for message in early:
        message.pending = False
        message.out.wait_send()
    f2.middle()
    b2.middle()
    gz[1].middle()
    gz[2].middle()
    f1[3].finish()
    b1[3].finish()

    gz[0].arrive()
    for h in (0, 1):
        gq[:, 64 * h:64 * h + 64] = gz[0].total(h).T.astype(BF)
    fetch(gq, gq_h)
    gz[3].arrive()
    for h in (0, 1):
        go[64 * h:64 * h + 64, :] = gz[3].total(h).astype(BF)
    fetch(go, go_h)
    f2.arrive()
    b2.arrive()
    for h in (0, 1):
        c = slice(h * HALF, (h + 1) * HALF)
        bo[:, c] = (tok[X, Y, :, c].astype(F32) + f2.total(h)).astype(BF)
        gt[:, c] = (cot[X, Y, :, c].astype(F32) + b2.total(h)).astype(BF)
    fetch(bo, bo_h)
    fetch(gt, gt_h)
    for a, ref, whole in ((1, gk, gk_h), (2, gv, gv_h)):
        gz[a].arrive()
        for h in (0, 1):
            ref[:, 64 * h:64 * h + 64] = gz[a].total(h).T.astype(BF)
        fetch(ref, whole)
    link.drain()
    for copy in copies[14:]:
        copy.wait()


def deliver(*refs):
    inputs, outputs, held, sems = refs[:6], refs[6:12], refs[12:18], refs[18]
    into = [pltpu.make_async_copy(inputs[n], held[n], sems.at[n]) for n in range(6)]
    out = [pltpu.make_async_copy(held[n], outputs[n], sems.at[6 + n]) for n in range(6)]
    for copy in into:
        copy.start()
    for n in range(6):
        into[n].wait()
        out[n].start()
    for copy in out:
        copy.wait()


def shards(tokens, cotangent, encoded, w_query, w_key, w_value, w_out, neigh_owner, neigh_row):
    any_ref = pl.BlockSpec(memory_space=pl.ANY)
    smem = pl.BlockSpec(memory_space=pltpu.SMEM)
    shape = jax.ShapeDtypeStruct
    results = pl.pallas_call(
        kernel,
        out_shape=(
            shape((16, D), BF), shape((16, D), BF), shape((TILE, HEAD), BF),
            shape((TILE, HEAD), BF), shape((TILE, HEAD), BF), shape((HEAD, TILE), BF),
        ),
        in_specs=[any_ref] * 7 + [smem] * 2,
        out_specs=(any_ref,) * 6,
        scratch_shapes=[
            pltpu.VMEM((16, 128, D), BF),
            pltpu.VMEM((4, 4, 16, D), BF),
            pltpu.VMEM((4, 4, 16, D), BF),
            pltpu.VMEM((D, HEAD), BF),
            pltpu.VMEM((D, 2 * HEAD), BF),
            pltpu.VMEM((HEAD, D), BF),
            pltpu.VMEM((16, 128, 256), BF),
            pltpu.VMEM((16, 128, 256), BF),
            pltpu.VMEM((16, 128, 256), BF),
            pltpu.VMEM((32, GROUP, 256), BF),
            pltpu.VMEM((32, 8, 128), F32),
            pltpu.VMEM((2, 128, 256), BF),
            pltpu.VMEM((2, 128, 256), BF),
            pltpu.VMEM((4, 4, 16, HEAD), F32),
            pltpu.VMEM((4, 4, 16, HEAD), F32),
            pltpu.VMEM((4, 4, 16, D), BF),
            pltpu.VMEM((4, 4, 16, D), BF),
            pltpu.VMEM((2, 5, 6, 16, HALF), BF),
            pltpu.VMEM((4, NSEQ, HEAD, TILE), BF),
            pltpu.VMEM((4, 4, HEAD, TILE), BF),
            pltpu.VMEM((4, 6, 64, TILE), BF),
            pltpu.VMEM((NSEQ, 256, 256), BF),
            pltpu.SMEM((16,), jnp.int32),
            pltpu.SMEM((16,), jnp.int32),
            pltpu.SMEM((16,), jnp.int32),
            pltpu.SMEM((8,), jnp.int32),
            pltpu.VMEM((16, D), BF),
            pltpu.VMEM((16, D), BF),
            pltpu.VMEM((TILE, HEAD), BF),
            pltpu.VMEM((TILE, HEAD), BF),
            pltpu.VMEM((TILE, HEAD), BF),
            pltpu.VMEM((HEAD, TILE), BF),
            pltpu.SemaphoreType.DMA((MESSAGES + 8,)),
            pltpu.SemaphoreType.DMA((MESSAGES + 8,)),
            pltpu.SemaphoreType.DMA((24,)),
        ],
        compiler_params=pltpu.CompilerParams(
            collective_id=0, has_side_effects=True, vmem_limit_bytes=60 * 1024 * 1024
        ),
        cost_estimate=pl.CostEstimate(flops=10_500_000_000, bytes_accessed=22_000_000, transcendentals=400_000),
    )(tokens, cotangent, encoded, w_query, w_key, w_value, w_out, neigh_owner.T, neigh_row.T)
    return pl.pallas_call(
        deliver,
        out_shape=tuple(shape(r.shape, r.dtype) for r in results),
        in_specs=[any_ref] * 6,
        out_specs=(any_ref,) * 6,
        scratch_shapes=[pltpu.VMEM(r.shape, r.dtype) for r in results] + [pltpu.SemaphoreType.DMA((12,))],
        compiler_params=pltpu.CompilerParams(vmem_limit_bytes=60 * 1024 * 1024),
    )(*results)


def solution(mesh):
    placed = (
        P(("seq", "enc", "dp"), None),
        P(("seq", "enc", "dp"), None),
        P("seq", None, None),
        P(None, ("enc", "dp")),
        P(None, ("enc", "dp")),
        P(None, ("enc", "dp")),
        P(("enc", "dp"), None),
        P(),
        P(),
    )
    return jax.shard_map(
        shards,
        mesh=mesh,
        in_specs=placed,
        out_specs=(
            P(("seq", "enc", "dp"), None),
            P(("seq", "enc", "dp"), None),
            P("seq", ("enc", "dp")),
            P("seq", ("enc", "dp")),
            P("seq", ("enc", "dp")),
            P(("enc", "dp"), "seq"),
        ),
        check_vma=False,
    )
```

```python
import math

import jax
import jax.numpy as jnp
from jax import lax
from jax.experimental import pallas as pl
from jax.experimental.pallas import tpu as pltpu
from jax.sharding import PartitionSpec as P

MESH = pl.DeviceIdType.MESH
BF = jnp.bfloat16
F32 = jnp.float32
D = 4096
HALF = D // 2
HEAD = 128
GROUP = 64
NSEQ = 8
RING = 4
TILE = D // NSEQ
MESSAGES = 188
SCALE = 1.0 / math.sqrt(HEAD)
NT = (((1,), (1,)), ((), ()))


def mm(a, b):
    return jnp.dot(a, b, preferred_element_type=F32)


def mm_t(a, b):
    return lax.dot_general(a, b, NT, preferred_element_type=F32)


class Link:
    def __init__(self, send, recv):
        self.send, self.recv, self.sent = send, recv, []

    def drain(self):
        for message in self.sent:
            if message.pending:
                message.pending = False
                message.out.wait_send()

    def message(self, src, dst, peer, land):
        index = len(self.sent)
        out = pltpu.make_async_remote_copy(
            src_ref=src, dst_ref=dst, send_sem=self.send.at[index], recv_sem=self.recv.at[index],
            device_id=peer, device_id_type=MESH)
        back = pltpu.make_async_remote_copy(
            src_ref=land, dst_ref=land, send_sem=self.send.at[index], recv_sem=self.recv.at[index],
            device_id=peer, device_id_type=MESH)
        made = Message(out, back)
        self.sent.append(made)
        return made


class Message:
    def __init__(self, out, back):
        self.out, self.back = out, back
        self.pending = False

    def start(self):
        self.pending = True
        self.out.start()

    def wait(self):
        self.back.wait_recv()


class Gather:
    def __init__(self, link, axis, me, at, own=None):
        right, left, far = (me + 1) % RING, (me + 3) % RING, (me + 2) % RING
        own = own or (lambda h: at(me, h))
        to_r, to_l = {axis: right}, {axis: left}
        self.r = [link.message(own(h), at(me, h), to_r, at(left, h)) for h in (0, 1)]
        self.l = [link.message(own(h), at(me, h), to_l, at(right, h)) for h in (0, 1)]
        self.fr = link.message(at(left, 0), at(left, 0), to_r, at(far, 0))
        self.fl = link.message(at(right, 1), at(right, 1), to_l, at(far, 1))

    def start(self):
        self.r[0].start()
        self.l[1].start()
        self.r[1].start()
        self.l[0].start()

    def forward(self):
        self.r[0].wait()
        self.fr.start()
        self.l[1].wait()
        self.fl.start()

    def near(self):
        self.r[1].wait()
        self.l[0].wait()

    def far(self):
        self.fr.wait()
        self.fl.wait()


class Reduce:
    def __init__(self, link, axis, me, part, buf):
        right, left, far = (me + 1) % RING, (me + 3) % RING, (me + 2) % RING
        to_r, to_l = {axis: right}, {axis: left}
        self.me, self.right, self.left, self.part, self.buf = me, right, left, part, buf
        self.r2 = link.message(part(far, 0), buf(0), to_r, buf(0))
        self.r1b = link.message(part(right, 0), buf(1), to_r, buf(1))
        self.r1a = link.message(part(right, 1), buf(2), to_r, buf(2))
        self.l2 = link.message(part(far, 1), buf(3), to_l, buf(3))
        self.l1b = link.message(part(left, 1), buf(4), to_l, buf(4))
        self.l1a = link.message(part(left, 0), buf(5), to_l, buf(5))

    def start_far(self):
        self.r2.start()
        self.l2.start()

    def start_right(self):
        self.r1a.start()

    def start_left(self):
        self.l1a.start()

    def add(self, ref, *bufs):
        total = ref[...].astype(F32)
        for index in bufs:
            total = total + self.buf(index)[...].astype(F32)
        ref[...] = total.astype(BF)

    def middle(self):
        self.r2.wait()
        self.add(self.part(self.right, 0), 0)
        self.r1b.start()
        self.l2.wait()
        self.add(self.part(self.left, 1), 3)
        self.l1b.start()

    def arrive(self):
        self.r1a.wait()
        self.l1a.wait()
        self.r1b.wait()
        self.l1b.wait()

    def total(self, h):
        first, second = ((1, 5), (2, 4))[h]
        total = self.part(self.me, h)[...].astype(F32)
        return total + self.buf(first)[...].astype(F32) + self.buf(second)[...].astype(F32)

    def finish(self):
        self.arrive()
        for h in (0, 1):
            self.part(self.me, h)[...] = self.total(h).astype(BF)


def kernel(
    tok_h, cot_h, enc_h, wq_h, wk_h, wv_h, wo_h, owner, row_of,
    bo_h, gt_h, gq_h, gk_h, gv_h, go_h,
    enc, tok, cot, wq, wkv, wo, own_kv, kv_s, kv_r, qd, stats, prev_s, prev_r, q_rows, d_rows,
    fwd, bwd, rx, grad, core_in, rz, dkv_t, plan_row, plan_win, plan_use, slots,
    bo, gt, gq, gk, gv, go, send, recv, local,
):
    S, X, Y = lax.axis_index("seq"), lax.axis_index("enc"), lax.axis_index("dp")
    Z, C = S // 2, S % 2
    other = Z * 2 + 1 - C
    link = Link(send, recv)

    copies = []

    def fetch(src, dst):
        copy = pltpu.make_async_copy(src, dst, local.at[len(copies)])
        copies.append(copy)
        copy.start()
        return copy

    barrier = pltpu.get_barrier_semaphore()
    peers = [{"enc": (X + 1) % RING}, {"enc": (X + 3) % RING}, {"dp": (Y + 1) % RING}, {"dp": (Y + 3) % RING}]
    peers += [{"seq": (S + d) % NSEQ} for d in range(1, NSEQ)]
    for peer in peers:
        pl.semaphore_signal(barrier, inc=1, device_id=peer, device_id_type=MESH)

    w_copies = [fetch(wk_h, wkv.at[:, pl.ds(0, HEAD)]), fetch(wv_h, wkv.at[:, pl.ds(HEAD, HEAD)])]
    e_copies = [fetch(enc_h.at[pl.ds(2 * c, 2)], enc.at[pl.ds(2 * c, 2)]) for c in range(8)]
    p_copies = [fetch(tok_h, tok.at[X, Y]), fetch(cot_h, cot.at[X, Y]), fetch(wq_h, wq), fetch(wo_h, wo)]

    def plan(d, carry):
        r = (S + d) % NSEQ
        count = jnp.int32(0)
        rows, wins, uses = [jnp.int32(0)] * 2, [jnp.int32(0)] * 2, [jnp.int32(0)] * 2
        for i in range(4):
            for j in range(2):
                hit = owner[j, 4 * r + i] == S
                row = row_of[j, 4 * r + i]
                for k in range(2):
                    here = jnp.logical_and(hit, count == k)
                    rows[k] = jnp.where(here, row, rows[k])
                    wins[k] = jnp.where(here, i, wins[k])
                    uses[k] = jnp.where(here, 1, uses[k])
                count = count + jnp.where(hit, 1, 0)
        for k in range(2):
            plan_row[2 * d + k] = rows[k]
            plan_win[2 * d + k] = wins[k]
            plan_use[2 * d + k] = uses[k]
        return carry

    lax.fori_loop(0, NSEQ, plan, 0)
    mine = []
    for i in range(4):
        for j in range(2):
            who = owner[j, 4 * S + i]
            rank = jnp.int32(0)
            for before in mine:
                rank = rank + jnp.where(before == who, 1, 0)
            slots[2 * i + j] = who * 2 + rank
            mine.append(who)

    def project(c):
        e_copies[c].wait()
        total = None
        for k in range(4):
            part = mm(enc[2 * c:2 * c + 2, :, k * 1024:(k + 1) * 1024].reshape(256, 1024), wkv[k * 1024:(k + 1) * 1024, :])
            total = part if total is None else total + part
        own_kv[2 * c:2 * c + 2] = total.astype(BF).reshape(2, 128, 256)

    for copy in w_copies:
        copy.wait()
    pl.semaphore_wait(barrier, len(peers))

    def cols(h):
        return pl.ds(h * HALF, HALF)

    xr, xl, xo = (X + 1) % RING, (X + 3) % RING, (X + 2) % RING
    yr, yl, yo = (Y + 1) % RING, (Y + 3) % RING, (Y + 2) % RING
    t_own = lambda h: tok_h.at[:, cols(h)]
    c_own = lambda h: cot_h.at[:, cols(h)]
    tx = Gather(link, "enc", X, lambda p, h: tok.at[p, Y, :, cols(h)], t_own)
    cy = Gather(link, "dp", Y, lambda p, h: cot.at[X, p, :, cols(h)], c_own)
    ty = [
        Gather(link, "dp", Y, lambda p, h, b=b: tok.at[b, p, :, cols(h)], t_own if n == 0 else None)
        for n, b in enumerate((X, xl, xr, xo))
    ]
    cx = [
        Gather(link, "enc", X, lambda p, h, b=b: cot.at[p, b, :, cols(h)], c_own if n == 0 else None)
        for n, b in enumerate((Y, yl, yr, yo))
    ]
    tx.start()
    cy.start()
    ty[0].start()
    cx[0].start()

    project(0)
    project(1)
    project(2)
    project(3)
    tx.forward()
    cy.forward()
    project(4)
    tx.near()
    ty[1].start()
    ty[2].start()
    cy.near()
    cx[1].start()
    cx[2].start()
    project(5)
    project(6)
    ty[0].forward()
    cx[0].forward()
    project(7)
    kv_messages = []
    for d in range(1, NSEQ):
        for k in range(2):
            kv_s[2 * d + k] = own_kv[plan_row[2 * d + k]]
        message = link.message(
            kv_s.at[pl.ds(2 * d, 2)], kv_r.at[pl.ds(2 * S, 2)], {"seq": (S + d) % NSEQ},
            kv_r.at[pl.ds(2 * ((S + NSEQ - d) % NSEQ), 2)])
        message.start()
        kv_messages.append(message)
    for k in range(2):
        kv_r[2 * S + k] = own_kv[plan_row[k]]
    tx.far()
    ty[3].start()
    cy.far()
    cx[3].start()
    for n in (1, 2):
        ty[n].forward()
        cx[n].forward()
    for copy in p_copies:
        copy.wait()
    ty[3].forward()
    cx[3].forward()
    for message in kv_messages:
        message.wait()
    for j in range(2):
        prev_s[j] = kv_r[slots[6 + j]]
    before = link.message(prev_s, prev_r, {"seq": (S + 1) % NSEQ}, prev_r)
    before.start()
    for n in range(4):
        ty[n].near()
        cx[n].near()
        if n:
            ty[n - 1].far()
            cx[n - 1].far()

    def project_rows(xs, ys):
        q, da = None, None
        for k in range(4):
            ks = slice(k * 1024, (k + 1) * 1024)
            rows = jnp.concatenate([tok[b, :, :, ks].reshape(GROUP, 1024) for b in xs], axis=0)
            part = mm(rows, wq[ks, :])
            q = part if q is None else q + part
            rows = jnp.concatenate([cot[:, b, :, ks].reshape(GROUP, 1024) for b in ys], axis=0)
            part = mm_t(rows, wo[:, ks])
            da = part if da is None else da + part
        for n, b in enumerate(xs):
            q_rows[b] = q[GROUP * n:GROUP * (n + 1)].reshape(4, 16, HEAD)
        for n, b in enumerate(ys):
            d_rows[:, b] = da[GROUP * n:GROUP * (n + 1)].reshape(4, 16, HEAD)

    project_rows((X, xl, xr), (Y, yl, yr))
    ty[3].far()
    cx[3].far()

    project_rows((xo,), (yo,))
    q, da = q_rows[...].reshape(256, HEAD), d_rows[...].reshape(256, HEAD)
    token = lax.broadcasted_iota(jnp.int32, (256, HEAD), 0)
    da = jnp.where(jnp.logical_or(token >= GROUP - 1, S > 0), da, 0.0)
    both = pltpu.roll(jnp.concatenate([q, da], axis=1), 1, 0).astype(BF)
    qd[pl.ds(4 * S, 4)] = both.reshape(4, GROUP, 256)

    def zb(p, h):
        return qd.at[pl.ds(4 * (2 * p + C) + 2 * h, 2)]

    def zo(p, h):
        return qd.at[pl.ds(4 * (2 * p + 1 - C) + 2 * h, 2)]

    zr, zl, zf = (Z + 1) % RING, (Z + 3) % RING, (Z + 2) % RING
    sibling = {"seq": other}

    class Column:
        pass

    def seq_peer(p):
        return {"seq": 2 * p + C}

    to_r, to_l = seq_peer(zr), seq_peer(zl)
    qg = Column()
    qg.r = [link.message(zb(Z, h), zb(Z, h), to_r, zb(zl, h)) for h in (0, 1)]
    qg.l = [link.message(zb(Z, h), zb(Z, h), to_l, zb(zr, h)) for h in (0, 1)]
    qg.fr = link.message(zb(zl, 0), zb(zl, 0), to_r, zb(zf, 0))
    qg.fl = link.message(zb(zr, 1), zb(zr, 1), to_l, zb(zf, 1))
    qs = {
        (p, h): link.message(zb(pos, h), zb(pos, h), sibling, zo(pos, h))
        for p, pos in (("me", Z), ("l", zl), ("r", zr), ("f", zf)) for h in (0, 1)
    }
    qg.l[0].start()
    qg.r[0].start()
    qg.l[1].start()
    qg.r[1].start()
    qs["me", 0].start()
    qs["me", 1].start()

    first_row = lax.broadcasted_iota(jnp.int32, (GROUP, 256), 0) == 0
    lane = lax.broadcasted_iota(jnp.int32, (GROUP, HEAD), 1)

    def window(block, kv0, kv1):
        pair = qd[4 * S + block]
        qw, dw = pair[:, :HEAD], pair[:, HEAD:]
        keys = jnp.concatenate([kv0[:, :HEAD], kv1[:, :HEAD]], axis=0)
        values = jnp.concatenate([kv0[:, HEAD:], kv1[:, HEAD:]], axis=0)
        scores = mm_t(qw, keys) * SCALE
        peak = jnp.max(scores, axis=-1, keepdims=True)
        expos = jnp.exp(scores - peak)
        norm = jnp.sum(expos, axis=-1, keepdims=True)
        probs = expos / norm
        out = mm(probs.astype(BF), values)
        d_probs = mm_t(dw, values)
        delta = jnp.sum(probs * d_probs, axis=-1, keepdims=True)
        d_scores = (probs * (d_probs - delta) * SCALE).astype(BF)
        dq = mm(d_scores, keys)
        column = jnp.where(lane == 0, peak + jnp.log(norm), delta)
        return jnp.concatenate([out, dq], axis=1), column

    def publish(block, column):
        stats[4 * S + block] = jnp.concatenate([column, column], axis=0).T[:8, :]

    parts = [None] * 4
    for i in range(3):
        parts[i + 1], column = window(i + 1, kv_r[slots[2 * i]], kv_r[slots[2 * i + 1]])
        publish(i + 1, column)
    last, last_column = window(0, kv_r[slots[6]], kv_r[slots[7]])
    before.wait()
    early, early_column = window(0, prev_r[0], prev_r[1])
    parts[0] = jnp.where(first_row, last, jnp.where(S > 0, early, 0.0))
    publish(0, jnp.where(first_row[:, :HEAD], last_column, early_column))
    done = pltpu.roll(jnp.concatenate(parts, axis=0), 255, 0).astype(BF)
    attn, dq = done[:, :HEAD], done[:, HEAD:]
    ford = (xo, xr, xl, X)
    bord = (yo, yr, yl, Y)
    f1 = [
        Reduce(link, "dp", Y, lambda p, h, b=b: fwd.at[b, p, :, cols(h)], lambda k, n=n: rx.at[0, n, k])
        for n, b in enumerate(ford)
    ]
    b1 = [
        Reduce(link, "enc", X, lambda p, h, b=b: bwd.at[p, b, :, cols(h)], lambda k, n=n: rx.at[1, n, k])
        for n, b in enumerate(bord)
    ]
    f2 = Reduce(link, "enc", X, lambda p, h: fwd.at[p, Y, :, cols(h)], lambda k: rx.at[0, 4, k])
    b2 = Reduce(link, "dp", Y, lambda p, h: bwd.at[X, p, :, cols(h)], lambda k: rx.at[1, 4, k])

    st_messages = []

    def stats_and_queries():
        for d in range(1, NSEQ):
            message = link.message(
                stats.at[pl.ds(4 * S, 4)], stats.at[pl.ds(4 * S, 4)], {"seq": (S + d) % NSEQ},
                stats.at[pl.ds(4 * ((S + NSEQ - d) % NSEQ), 4)])
            message.start()
            st_messages.append(message)

    def head_sum(ref, rings, h, tile):
        for n in range(4 * h, 4 * h + 4):
            c = slice(n * TILE, (n + 1) * TILE)
            ref[:, :, :, c] = tile(c).astype(BF).reshape(4, 4, 16, TILE)
        for r in rings:
            (r.l2 if h else r.r2).start()
        for r in rings[:1]:
            (r.r1a if h else r.l1a).start()

    stats_and_queries()
    for h in (0, 1):
        head_sum(fwd, f1, h, lambda c: mm(attn, wo[:, c]))
        head_sum(bwd, b1, h, lambda c: mm_t(dq, wq[c, :]))
        if h == 0:
            qg.l[0].wait()
            qs["r", 0].start()
            qg.r[0].wait()
            qg.fr.start()
            qg.l[1].wait()
            qg.fl.start()
            qg.r[1].wait()
            qs["r", 1].start()
            qs["l", 0].start()
            qs["l", 1].start()

    early = [m for m in link.sent if m.pending and m not in [r.r2 for r in f1 + b1] + [r.l2 for r in f1 + b1] + [r.r1a for r in f1 + b1] + [r.l1a for r in f1 + b1]]

    gc = [
        [
            link.message(grad.at[a, 2 * ((Z + w) % RING) + 1 - C], core_in.at[a, (Z + w) % RING], sibling, core_in.at[a, (Z + w) % RING])
            for w in (2, 1, 3, 0)
        ]
        for a in range(4)
    ]

    def zpart(a):
        return lambda p, h: grad.at[a, 2 * p + C, pl.ds(64 * h, 64), :]

    class ZReduce(Reduce):
        def __init__(self, a):
            part, buf = zpart(a), lambda k: rz.at[a, k]
            self.me, self.right, self.left, self.part, self.buf = Z, zr, zl, part, buf
            self.r2 = link.message(part(zf, 0), buf(0), to_r, buf(0))
            self.r1b = link.message(part(zr, 0), buf(1), to_r, buf(1))
            self.r1a = link.message(part(zr, 1), buf(2), to_r, buf(2))
            self.l2 = link.message(part(zf, 1), buf(3), to_l, buf(3))
            self.l1b = link.message(part(zl, 1), buf(4), to_l, buf(4))
            self.l1a = link.message(part(zl, 0), buf(5), to_l, buf(5))

    gz = [ZReduce(a) for a in range(4)]

    def core_sum(a, n):
        gc[a][n].wait()
        p = (Z + (2, 1, 3, 0)[n]) % RING
        total = grad[a, 2 * p + C].astype(F32) + core_in[a, p].astype(F32)
        grad[a, 2 * p + C] = total.astype(BF)
        if n == 0:
            gz[a].start_far()
        elif n == 1:
            gz[a].start_right()
        elif n == 2:
            gz[a].start_left()

    def token_gradient(a, left, right):
        left_t = left.astype(F32).T.astype(BF)
        for n in range(NSEQ):
            c = slice(n * TILE, (n + 1) * TILE)
            grad[a, n] = mm(left_t, right[:, :, :, c].reshape(256, TILE)).astype(BF)
        for n in range(4):
            gc[a][n].start()

    token_gradient(3, attn, cot)
    qg.fr.wait()
    qs["f", 0].start()
    qg.fl.wait()
    qs["f", 1].start()
    token_gradient(0, dq, tok)
    f1[0].middle()
    b1[0].middle()
    for r in (f1[1], b1[1], f1[2], b1[2], f1[3], b1[3]):
        r.start_right()
        r.start_left()
    for n in range(4):
        core_sum(3, n)
    f1[1].middle()
    b1[1].middle()
    for n in range(4):
        core_sum(0, n)
    for message in qs.values():
        message.wait()
    for message in st_messages:
        message.wait()

    first_lane = lax.broadcasted_iota(jnp.int32, (8, HEAD), 1) == 0

    def slot(d, k):
        index = 2 * d + k
        r = (S + d) % NSEQ
        b, i, use = plan_row[index], plan_win[index], plan_use[index]
        ahead = qd[(4 * r + i + 1) % 32].astype(F32)
        pair = jnp.where(jnp.logical_and(first_row, i == 3), qd[4 * r].astype(F32), ahead).astype(BF)
        qw, dw = pair[:, :HEAD], pair[:, HEAD:]
        kv = own_kv[b]
        stat = jnp.where(jnp.logical_and(first_lane, i == 3), stats[4 * r], stats[(4 * r + i + 1) % 32])
        scores = mm_t(kv[:, :HEAD], qw) * SCALE
        probs = jnp.where(use > 0, jnp.exp(scores - stat[0:1, :GROUP]), 0.0)
        d_probs = mm_t(kv[:, HEAD:], dw)
        d_scores = probs * (d_probs - stat[1:2, :GROUP]) * SCALE
        d_keys = mm(d_scores.astype(BF), qw)
        d_values = mm(probs.astype(BF), dw)
        return jnp.concatenate([d_keys, d_values], axis=1).T.astype(BF)

    def slot_pair(d, carry):
        dkv_t[d] = jnp.concatenate([slot(d, 0), slot(d, 1)], axis=1)
        return carry

    lax.fori_loop(0, NSEQ, slot_pair, 0)
    gz[3].middle()
    f1[2].middle()
    b1[2].middle()

    def kv_tile(n):
        c = pl.ds(pl.multiple_of(n * TILE, TILE), TILE)
        total = None
        for d in range(NSEQ):
            rows = jnp.concatenate([enc[plan_row[2 * d], :, c], enc[plan_row[2 * d + 1], :, c]], axis=0)
            part = mm(dkv_t[d], rows)
            total = part if total is None else total + part
        total = total.astype(BF)
        grad[1, n] = total[:HEAD]
        grad[2, n] = total[HEAD:]

    for n, w in enumerate((2, 1, 3, 0)):
        kv_tile(2 * ((Z + w) % RING) + 1 - C)
        gc[1][n].start()
        gc[2][n].start()
        kv_tile(2 * ((Z + w) % RING) + C)
        core_sum(1, n)
        core_sum(2, n)
        if n == 0:
            gz[0].middle()
        if n == 0:
            f1[0].finish()
            f2.start_far()
            b1[0].finish()
            b2.start_far()
            f1[3].middle()
            b1[3].middle()
        if n == 1:
            f1[1].finish()
            f2.start_right()
            b1[1].finish()
            b2.start_right()
        if n == 2:
            f1[2].finish()
            f2.start_left()
            b1[2].finish()
            b2.start_left()
    for message in early:
        message.pending = False
        message.out.wait_send()
    f2.middle()
    b2.middle()
    gz[1].middle()
    gz[2].middle()
    f1[3].finish()
    b1[3].finish()

    gz[0].arrive()
    for h in (0, 1):
        gq[:, 64 * h:64 * h + 64] = gz[0].total(h).T.astype(BF)
    fetch(gq, gq_h)
    gz[3].arrive()
    for h in (0, 1):
        go[64 * h:64 * h + 64, :] = gz[3].total(h).astype(BF)
    fetch(go, go_h)
    f2.arrive()
    b2.arrive()
    for h in (0, 1):
        c = slice(h * HALF, (h + 1) * HALF)
        bo[:, c] = (tok[X, Y, :, c].astype(F32) + f2.total(h)).astype(BF)
        gt[:, c] = (cot[X, Y, :, c].astype(F32) + b2.total(h)).astype(BF)
    fetch(bo, bo_h)
    fetch(gt, gt_h)
    for a, ref, whole in ((1, gk, gk_h), (2, gv, gv_h)):
        gz[a].arrive()
        for h in (0, 1):
            ref[:, 64 * h:64 * h + 64] = gz[a].total(h).T.astype(BF)
        fetch(ref, whole)
    link.drain()
    for copy in copies[14:]:
        copy.wait()


def deliver(*refs):
    inputs, outputs, held, sems = refs[:6], refs[6:12], refs[12:18], refs[18]
    into = [pltpu.make_async_copy(inputs[n], held[n], sems.at[n]) for n in range(6)]
    out = [pltpu.make_async_copy(held[n], outputs[n], sems.at[6 + n]) for n in range(6)]
    for copy in into:
        copy.start()
    for n in range(6):
        into[n].wait()
        out[n].start()
    for copy in out:
        copy.wait()


def shards(tokens, cotangent, encoded, w_query, w_key, w_value, w_out, neigh_owner, neigh_row):
    any_ref = pl.BlockSpec(memory_space=pl.ANY)
    smem = pl.BlockSpec(memory_space=pltpu.SMEM)
    shape = jax.ShapeDtypeStruct
    results = pl.pallas_call(
        kernel,
        out_shape=(
            shape((16, D), BF), shape((16, D), BF), shape((TILE, HEAD), BF),
            shape((TILE, HEAD), BF), shape((TILE, HEAD), BF), shape((HEAD, TILE), BF),
        ),
        in_specs=[any_ref] * 7 + [smem] * 2,
        out_specs=(any_ref,) * 6,
        scratch_shapes=[
            pltpu.VMEM((16, 128, D), BF),
            pltpu.VMEM((4, 4, 16, D), BF),
            pltpu.VMEM((4, 4, 16, D), BF),
            pltpu.VMEM((D, HEAD), BF),
            pltpu.VMEM((D, 2 * HEAD), BF),
            pltpu.VMEM((HEAD, D), BF),
            pltpu.VMEM((16, 128, 256), BF),
            pltpu.VMEM((16, 128, 256), BF),
            pltpu.VMEM((16, 128, 256), BF),
            pltpu.VMEM((32, GROUP, 256), BF),
            pltpu.VMEM((32, 8, 128), F32),
            pltpu.VMEM((2, 128, 256), BF),
            pltpu.VMEM((2, 128, 256), BF),
            pltpu.VMEM((4, 4, 16, HEAD), F32),
            pltpu.VMEM((4, 4, 16, HEAD), F32),
            pltpu.VMEM((4, 4, 16, D), BF),
            pltpu.VMEM((4, 4, 16, D), BF),
            pltpu.VMEM((2, 5, 6, 16, HALF), BF),
            pltpu.VMEM((4, NSEQ, HEAD, TILE), BF),
            pltpu.VMEM((4, 4, HEAD, TILE), BF),
            pltpu.VMEM((4, 6, 64, TILE), BF),
            pltpu.VMEM((NSEQ, 256, 256), BF),
            pltpu.SMEM((16,), jnp.int32),
            pltpu.SMEM((16,), jnp.int32),
            pltpu.SMEM((16,), jnp.int32),
            pltpu.SMEM((8,), jnp.int32),
            pltpu.VMEM((16, D), BF),
            pltpu.VMEM((16, D), BF),
            pltpu.VMEM((TILE, HEAD), BF),
            pltpu.VMEM((TILE, HEAD), BF),
            pltpu.VMEM((TILE, HEAD), BF),
            pltpu.VMEM((HEAD, TILE), BF),
            pltpu.SemaphoreType.DMA((MESSAGES + 8,)),
            pltpu.SemaphoreType.DMA((MESSAGES + 8,)),
            pltpu.SemaphoreType.DMA((24,)),
        ],
        compiler_params=pltpu.CompilerParams(
            collective_id=0, has_side_effects=True, vmem_limit_bytes=60 * 1024 * 1024
        ),
        cost_estimate=pl.CostEstimate(flops=10_500_000_000, bytes_accessed=22_000_000, transcendentals=400_000),
    )(tokens, cotangent, encoded, w_query, w_key, w_value, w_out, neigh_owner.T, neigh_row.T)
    return pl.pallas_call(
        deliver,
        out_shape=tuple(shape(r.shape, r.dtype) for r in results),
        in_specs=[any_ref] * 6,
        out_specs=(any_ref,) * 6,
        scratch_shapes=[pltpu.VMEM(r.shape, r.dtype) for r in results] + [pltpu.SemaphoreType.DMA((12,))],
        compiler_params=pltpu.CompilerParams(vmem_limit_bytes=60 * 1024 * 1024),
    )(*results)


def solution(mesh):
    placed = (
        P(("seq", "enc", "dp"), None),
        P(("seq", "enc", "dp"), None),
        P("seq", None, None),
        P(None, ("enc", "dp")),
        P(None, ("enc", "dp")),
        P(None, ("enc", "dp")),
        P(("enc", "dp"), None),
        P(),
        P(),
    )
    return jax.shard_map(
        shards,
        mesh=mesh,
        in_specs=placed,
        out_specs=(
            P(("seq", "enc", "dp"), None),
            P(("seq", "enc", "dp"), None),
            P("seq", ("enc", "dp")),
            P("seq", ("enc", "dp")),
            P("seq", ("enc", "dp")),
            P(("enc", "dp"), "seq"),
        ),
        check_vma=False,
    )
```
